256 devices in a mesh: member: 16 (over z_lo, x, core), grid: 16 (over y, z_hi).
Axes of the slice: x: 4, y: 4, z: 8 (z_hi: 4, z_lo: 2; z = z_hi * 2 + z_lo), core: 2. Of those that a mesh axis runs over, the one named last changes fastest.
Arguments:
- latent: float32 [16, 32768, 512], P('member', 'grid'), may hold values from -6 to 6
- dec_weight: float32 [512, 32], replicated, may hold values from -0.25 to 0.25
- dec_bias: float32 [32], replicated, may hold values from -3 to 3
- target: float32 [32, 32768], P(None, 'grid'), may hold values from -9 to 9
- area: float32 [32768], P('grid'), may hold values from 0.05 to 1.6, as said below
- var_weight: float32 [32], replicated, may hold values from 0.5 to 4
Outputs:
- loss: float32 [], replicated
- grad_latent: float32 [16, 32768, 512], P('member', 'grid')
- grad_weight: float32 [512, 32], replicated
- grad_bias: float32 [32], replicated
The draws below stay inside these ranges and needn't reach their ends.
Inputs may be any that keep to these rules, and one draw needn't show every extreme that they name: Positive area weights of the window's nodes.
All inputs are finite; a program needn't handle non-finite values.
Results may differ from the reference program's by a relative error of at most 0.00017.
Values sent between devices are 32-bit elements; how exact they have to be, the bound alone decides.
No kernel may reach another device: no remote copies, remote signals or barrier semaphores. Data moves between devices by JAX's collectives and lax.ppermute only.
A program may use at most 64 MiB of HBM per device.

```python
import math
import jax
import jax.numpy as jnp
from jax import lax

MEMBERS = 16
LATENT = 512
VARS = 32
NODES = 32768


def draw_area(key, part):
    key = jax.random.fold_in(key, 7)
    position = jnp.arange(NODES).astype(jnp.float32)
    latitude = (position + 0.5) / NODES * (80.0 / 180.0 * math.pi)
    rough = jax.random.uniform(key, (NODES,), jnp.float32, 0.7, 1.3)
    return jnp.cos(latitude) * rough


def shard_levels(rng, extent, pieces, least, largest):
    loudness, own = 1.0, jax.random.fold_in(rng, 6)
    for dim, shards_of in pieces:
        steps = jnp.exp(jax.random.uniform(jax.random.fold_in(own, dim), (shards_of,), jnp.float32, least / len(pieces), largest / len(pieces)))
        loudness = loudness * jnp.repeat(steps, extent[dim] // shards_of).reshape([-1 if axis == dim else 1 for axis in range(len(extent))])
    return loudness


def normal_values(key, extent, scale, most, pieces=(), dtype=jnp.bfloat16):
    values = jax.random.normal(key, extent, jnp.float32) * scale
    if len(pieces) > 0:
        values = shard_levels(key, extent, pieces, -0.22, 0.18) * values
    return jnp.clip(values, min=-most, max=most).astype(dtype)


def setup_inputs(seed: int = 0) -> dict:
    seeds = jax.random.split(jax.random.key(seed), 7)
    latent = normal_values(seeds[0], (MEMBERS, NODES, LATENT), 1.0, 6.0, ((0, 16), (1, 16)), jnp.float32)
    dec_weight = normal_values(seeds[1], (LATENT, VARS), LATENT ** -0.5, 0.25, (), jnp.float32)
    dec_bias = normal_values(seeds[2], (VARS,), 0.5, 3.0, (), jnp.float32)
    target = normal_values(seeds[3], (VARS, NODES), 1.5, 9.0, ((1, 16),), jnp.float32)
    area = draw_area(jax.random.fold_in(seeds[6], 71), 0)
    var_weight = jnp.clip(jnp.exp(jax.random.uniform(seeds[5], (VARS,), jnp.float32, math.log(0.5), math.log(4.0))), 0.5, 4.0)
    return dict(latent=latent, dec_weight=dec_weight, dec_bias=dec_bias, target=target, area=area, var_weight=var_weight)


SMOOTHING = 0.1

def smooth_abs(spread):
    return jnp.sqrt(spread * spread + SMOOTHING * SMOOTHING)

def smooth_slope(spread):
    return spread / smooth_abs(spread)

def reference(latent, dec_weight, dec_bias, target, area, var_weight):
    highest = lax.Precision.HIGHEST
    fields = jnp.einsum('mnk,kv->mvn', latent, dec_weight, precision=highest) + dec_bias[None, :, None]
    area_mean = jnp.sum(area) / NODES
    node_scale = var_weight[:, None] * (area / area_mean)[None, :]
    to_target = fields - target[None]
    target_term = lax.optimization_barrier(jnp.sum(smooth_abs(to_target), 0)) / MEMBERS
    target_slope = smooth_slope(to_target) / MEMBERS
    pair_sum = jnp.zeros(target.shape, jnp.float32)
    rows = []
    for first in range(MEMBERS):
        row_slope = jnp.zeros(target.shape, jnp.float32)
        for second in range(MEMBERS):
            if second != first:
                spread = fields[first] - fields[second]
                row_slope = row_slope + smooth_slope(spread)
                if second > first:
                    pair_sum = pair_sum + smooth_abs(spread)
        rows.append(row_slope)
    pair_slope = jnp.stack(rows, 0)
    norm_pairs = float(MEMBERS * (MEMBERS - 1))
    crps = target_term - pair_sum / norm_pairs
    loss = jnp.sum(node_scale * crps) / NODES
    field_grad = node_scale[None] * (target_slope - pair_slope / norm_pairs)
    grad_latent = jnp.einsum('mvn,kv->mnk', field_grad, dec_weight, precision=highest)
    grad_weight = jnp.einsum('mnk,mvn->kv', latent, field_grad, precision=highest) / NODES
    grad_bias = lax.optimization_barrier(jnp.sum(field_grad, (0, 2))) / NODES
    return (loss, grad_latent, grad_weight, grad_bias)
```

```python
import jax
import jax.numpy as jnp
from jax import lax
from jax.experimental import pallas as pl
from jax.experimental.pallas import tpu as pltpu
from jax.sharding import Mesh, PartitionSpec as P

MEMBERS = 16
LATENT = 512
VARS = 32
SMOOTHING = 0.1
LANES = 128
BLOCK = 512
CHUNKS = BLOCK // LANES
HALF = LATENT // 2
ROWS = VARS * HALF // LANES
EXTRA = 8
MEMBER = ("zl", "x", "c")
GRID = ("y", "zh")
F32 = jnp.float32
BF16 = jnp.bfloat16


def params(mib):
    return pltpu.CompilerParams(vmem_limit_bytes=mib * 1024 * 1024)


def split(a):
    hi = a.astype(BF16)
    return hi, (a - hi.astype(F32)).astype(BF16)


def dot(a, b, over):
    return lax.dot_general(a, b, (((over[0],), (over[1],)), ((), ())), preferred_element_type=F32)


def columns(row):
    return jnp.transpose(jnp.broadcast_to(row, (LANES, VARS)))


def decode_kernel(x_ref, w_ref, b_ref, out_ref):
    xh, xl = split(x_ref[...])
    wh, wl = split(w_ref[...])
    both = dot(jnp.concatenate([wh, wl], 0), xh, (1, 1))
    f = both[:VARS] + both[VARS:] + dot(wh, xl, (1, 1))
    bias = columns(b_ref[...])
    for i in range(CHUNKS):
        out_ref[i] = f[:, i * LANES : (i + 1) * LANES] + bias


def crps_kernel(at_ref, f_ref, t_ref, a_ref, v_ref, grad_ref, extra_ref):
    area = a_ref[pl.ds(at_ref[0], 1), :]
    scale = columns(v_ref[...]) * area
    sums = []
    loss = jnp.zeros((8, LANES), F32)
    for r in range(0, VARS, 8):
        rows = slice(r, r + 8)
        t = t_ref[rows, :]
        f = [f_ref[m, rows, :] for m in range(MEMBERS)]
        slope = [None] * MEMBERS
        near = jnp.zeros((8, LANES), F32)
        pairs = jnp.zeros((8, LANES), F32)
        total = [jnp.zeros((8, LANES), F32) for _ in range(MEMBERS)]
        for i in range(MEMBERS):
            d = f[i] - t
            q = d * d + SMOOTHING * SMOOTHING
            inv = lax.rsqrt(q)
            near = near + q * inv
            slope[i] = d * inv
            for j in range(i + 1, MEMBERS):
                d = f[i] - f[j]
                q = d * d + SMOOTHING * SMOOTHING
                inv = lax.rsqrt(q)
                pairs = pairs + q * inv
                s = d * inv
                total[i] = total[i] + s
                total[j] = total[j] - s
        norm = 1.0 / (MEMBERS * (MEMBERS - 1))
        here = scale[rows]
        loss = loss + here * (near * (1.0 / MEMBERS) - pairs * norm)
        fsum = jnp.zeros((8, LANES), F32)
        for m in range(MEMBERS):
            g = here * (slope[m] * (1.0 / MEMBERS) - total[m] * norm)
            grad_ref[m, rows, :] = g
            fsum = fsum + g
        sums.append(fsum)
    extra_ref[...] = jnp.zeros((EXTRA, LANES), F32)
    bias = jnp.sum(jnp.transpose(jnp.concatenate(sums, 0)), 0, keepdims=True)
    extra_ref[0:1, 0:VARS] = bias
    extra_ref[1:2, :] = jnp.sum(loss, 0, keepdims=True)
    extra_ref[2:3, :] = area


def weight_kernel(c_ref, g_ref, x_ref, e_ref, own_ref, other_ref, acc_ref):
    step = pl.program_id(0)
    g = jnp.concatenate([g_ref[i] for i in range(CHUNKS)], 1)
    gh, gl = split(g)
    xh, xl = split(x_ref[...])
    both = dot(jnp.concatenate([gh, gl], 0), xh, (1, 0))
    part = both[:VARS] + both[VARS:] + dot(gh, xl, (1, 0))

    @pl.when(step == 0)
    def _():
        acc_ref[...] = part

    @pl.when(step > 0)
    def _():
        acc_ref[...] += part

    @pl.when(step == pl.num_programs(0) - 1)
    def _():
        first = c_ref[0] == 0
        for i in range(HALF // LANES):
            rows = slice(i * VARS, (i + 1) * VARS)
            low = acc_ref[:, i * LANES : (i + 1) * LANES]
            high = acc_ref[:, HALF + i * LANES : HALF + (i + 1) * LANES]
            own_ref[rows, :] = jnp.where(first, low, high)
            other_ref[rows, :] = jnp.where(first, high, low)
        own_ref[ROWS:, :] = e_ref[...]
        other_ref[ROWS:, :] = e_ref[...]


def pair_kernel(a_ref, b_ref, out_ref):
    s = a_ref[...] + b_ref[...]
    for i in range(out_ref.shape[0]):
        out_ref[i] = s


def fold_kernel(in_ref, out_ref):
    s = in_ref[0]
    for i in range(1, in_ref.shape[0]):
        s = s + in_ref[i]
    for i in range(out_ref.shape[0]):
        out_ref[i] = s


def last_kernel(in_ref, w_ref, e_ref):
    s = in_ref[0]
    for i in range(1, in_ref.shape[0]):
        s = s + in_ref[i]
    e = s[ROWS:]
    area = jnp.sum(e[2:3], 1, keepdims=True)
    w_ref[...] = s[:ROWS] / area
    e_ref[0:1, :] = e[0:1] / area
    e_ref[1:2, :] = jnp.broadcast_to(jnp.sum(e[1:2], 1, keepdims=True) / area, (1, LANES))
    e_ref[2:3, :] = jnp.broadcast_to(1.0 / area, (1, LANES))
    e_ref[3:, :] = jnp.zeros((EXTRA - 3, LANES), F32)


def latent_kernel(nodes, g_ref, w_ref, e_ref, out_ref):
    inv = e_ref[2:3, :] * float(nodes)
    g = jnp.concatenate([g_ref[i] * inv for i in range(CHUNKS)], 1)
    gh, gl = split(g)
    wh, wl = split(w_ref[...])
    out_ref[...] = dot(jnp.concatenate([gh, gl, gh], 0), jnp.concatenate([wh, wh, wl], 0), (0, 0))


def whole(shape):
    return pl.BlockSpec(shape, lambda *_: (0,) * len(shape))


def shape(*s):
    return jax.ShapeDtypeStruct(s, F32)


def body(latent, dec_weight, dec_bias, target, area, var_weight):
    slab = area.shape[0]
    nodes = slab * lax.axis_size("y") * lax.axis_size("zh")
    steps = slab // BLOCK
    x = latent.reshape(slab, LATENT)
    wt = dec_weight.T
    me = lax.axis_index(MEMBER).astype(jnp.int32).reshape(1)
    core = lax.axis_index("c").astype(jnp.int32).reshape(1)

    fields = pl.pallas_call(
        decode_kernel,
        out_shape=shape(MEMBERS, VARS, LANES),
        grid=(steps,),
        in_specs=[
            pl.BlockSpec((BLOCK, LATENT), lambda i: (i, 0)),
            whole((VARS, LATENT)),
            whole((1, VARS)),
        ],
        out_specs=pl.BlockSpec((CHUNKS, VARS, LANES), lambda i: (i, 0, 0)),
        compiler_params=params(24),
    )(x, wt, dec_bias.reshape(1, VARS))

    fields = lax.all_to_all(fields, MEMBER, 0, 0)

    grads, extra = pl.pallas_call(
        crps_kernel,
        out_shape=(shape(MEMBERS, VARS, LANES), shape(EXTRA, LANES)),
        grid_spec=pltpu.PrefetchScalarGridSpec(
            num_scalar_prefetch=1,
            grid=(1,),
            in_specs=[
                whole((MEMBERS, VARS, LANES)),
                pl.BlockSpec((VARS, LANES), lambda i, at: (0, at[0])),
                whole((slab // LANES, LANES)),
                whole((1, VARS)),
            ],
            out_specs=(whole((MEMBERS, VARS, LANES)), whole((EXTRA, LANES))),
        ),
        compiler_params=params(16),
    )(me, fields, target, area.reshape(slab // LANES, LANES), var_weight.reshape(1, VARS))

    grads = lax.all_to_all(grads, MEMBER, 0, 0)

    own, other = pl.pallas_call(
        weight_kernel,
        out_shape=(shape(ROWS + EXTRA, LANES),) * 2,
        grid_spec=pltpu.PrefetchScalarGridSpec(
            num_scalar_prefetch=1,
            grid=(steps,),
            in_specs=[
                pl.BlockSpec((CHUNKS, VARS, LANES), lambda i, c: (i, 0, 0)),
                pl.BlockSpec((BLOCK, LATENT), lambda i, c: (i, 0)),
                whole((EXTRA, LANES)),
            ],
            out_specs=(whole((ROWS + EXTRA, LANES)),) * 2,
            scratch_shapes=[pltpu.VMEM((VARS, LATENT), F32)],
        ),
        compiler_params=params(24),
    )(core, grads, x, extra)

    swap = [(0, 1), (1, 0)]
    came = lax.ppermute(other, "c", swap)
    plane = lax.axis_size("x") * lax.axis_size("y")
    depth = lax.axis_size("zl") * lax.axis_size("zh")
    parts = pl.pallas_call(
        pair_kernel, out_shape=shape(plane, ROWS + EXTRA, LANES), compiler_params=params(16)
    )(own, came)
    parts = lax.all_to_all(parts, ("x", "y"), 0, 0)
    parts = pl.pallas_call(
        fold_kernel, out_shape=shape(depth, ROWS + EXTRA, LANES), compiler_params=params(16)
    )(parts)
    parts = lax.all_to_all(parts, ("zl", "zh"), 0, 0)
    mine, extra = pl.pallas_call(
        last_kernel, out_shape=(shape(ROWS, LANES), shape(EXTRA, LANES)), compiler_params=params(16)
    )(parts)
    theirs = lax.ppermute(mine, "c", swap)

    grad_latent = pl.pallas_call(
        lambda *refs: latent_kernel(nodes, *refs),
        out_shape=shape(slab, LATENT),
        grid=(steps,),
        in_specs=[
            pl.BlockSpec((CHUNKS, VARS, LANES), lambda i: (i, 0, 0)),
            whole((VARS, LATENT)),
            whole((EXTRA, LANES)),
        ],
        out_specs=pl.BlockSpec((BLOCK, LATENT), lambda i: (i, 0)),
        compiler_params=params(24),
        cost_estimate=pl.CostEstimate(flops=6 * slab * VARS * LATENT, bytes_accessed=4 * slab * LATENT, transcendentals=0),
    )(grads, wt, extra)

    first = core[0] == 0
    low = jnp.where(first, mine, theirs)
    high = jnp.where(first, theirs, mine)
    weight = jnp.concatenate([low[:VARS], low[VARS:], high[:VARS], high[VARS:]], 1).T
    return extra[1, 0], grad_latent[None], weight, extra[0, :VARS]


def solution(mesh):
    shaped = Mesh(mesh.devices.reshape(2, 4, 2, 4, 4), MEMBER + GRID)
    return jax.shard_map(
        body,
        mesh=shaped,
        in_specs=(P(MEMBER, GRID, None), P(), P(), P(None, GRID), P(GRID), P()),
        out_specs=(P(), P(MEMBER, GRID, None), P(), P()),
        check_vma=False,
    )
```

```python
import jax
import jax.numpy as jnp
from jax import lax
from jax.experimental import pallas as pl
from jax.experimental.pallas import tpu as pltpu
from jax.sharding import Mesh, PartitionSpec as P

MEMBERS = 16
LATENT = 512
VARS = 32
SMOOTHING = 0.1
LANES = 128
BLOCK = 512
CHUNKS = BLOCK // LANES
HALF = LATENT // 2
ROWS = VARS * HALF // LANES
EXTRA = 8
MEMBER = ("zl", "x", "c")
GRID = ("y", "zh")
F32 = jnp.float32
BF16 = jnp.bfloat16
VMEM = pl.BlockSpec(memory_space=pltpu.VMEM)
SMEM = pl.BlockSpec(memory_space=pltpu.SMEM)
HBM = pl.BlockSpec(memory_space=pltpu.HBM)


def in_hbm(a):
    return pltpu.with_memory_space_constraint(a, pltpu.HBM)


def params(mib):
    return pltpu.CompilerParams(vmem_limit_bytes=mib * 1024 * 1024)


def split(a):
    hi = a.astype(BF16)
    return hi, (a - hi.astype(F32)).astype(BF16)


def dot(a, b, over):
    return lax.dot_general(a, b, (((over[0],), (over[1],)), ((), ())), preferred_element_type=F32)


def columns(row):
    return jnp.transpose(jnp.broadcast_to(row, (LANES, VARS)))


def decode_kernel(me_ref, core_ref, x_hbm, w_hbm, b_hbm, out_ref, x_ref, w_ref, b_ref, sems, more):
    first = [
        pltpu.make_async_copy(w_hbm, w_ref, more.at[0]),
        pltpu.make_async_copy(b_hbm, b_ref, more.at[1]),
    ]
    for copy in first:
        copy.start()
    copies = []
    for i in range(x_ref.shape[0] // BLOCK):
        rows = pl.ds(i * BLOCK, BLOCK)
        copies.append(pltpu.make_async_copy(x_hbm.at[rows], x_ref.at[rows], sems.at[i]))
        copies[-1].start()
    for copy in first:
        copy.wait()
    wh, wl = split(w_ref[...])
    both = jnp.concatenate([wh, wl], 0)
    bias = columns(b_ref[...])
    for i, copy in enumerate(copies):
        copy.wait()
        rows = slice(i * BLOCK, (i + 1) * BLOCK)
        xh, xl = split(x_ref[rows, :])
        f = dot(both, xh, (1, 1))
        f = f[:VARS] + f[VARS:] + dot(wh, xl, (1, 1))
        for j in range(CHUNKS):
            out_ref[i * CHUNKS + j] = f[:, j * LANES : (j + 1) * LANES] + bias


def crps_kernel(at_ref, f_ref, t_ref, a_ref, v_ref, grad_ref, extra_ref):
    area = a_ref[pl.ds(at_ref[0], 1), :]
    scale = columns(v_ref[...]) * area
    sums = []
    loss = jnp.zeros((8, LANES), F32)
    for r in range(0, VARS, 8):
        rows = slice(r, r + 8)
        t = t_ref[rows, :]
        f = [f_ref[m, rows, :] for m in range(MEMBERS)]
        slope = [None] * MEMBERS
        near = jnp.zeros((8, LANES), F32)
        pairs = jnp.zeros((8, LANES), F32)
        total = [jnp.zeros((8, LANES), F32) for _ in range(MEMBERS)]
        for i in range(MEMBERS):
            d = f[i] - t
            q = d * d + SMOOTHING * SMOOTHING
            inv = lax.rsqrt(q)
            near = near + q * inv
            slope[i] = d * inv
            for j in range(i + 1, MEMBERS):
                d = f[i] - f[j]
                q = d * d + SMOOTHING * SMOOTHING
                inv = lax.rsqrt(q)
                pairs = pairs + q * inv
                s = d * inv
                total[i] = total[i] + s
                total[j] = total[j] - s
        norm = 1.0 / (MEMBERS * (MEMBERS - 1))
        here = scale[rows]
        loss = loss + here * (near * (1.0 / MEMBERS) - pairs * norm)
        fsum = jnp.zeros((8, LANES), F32)
        for m in range(MEMBERS):
            g = here * (slope[m] * (1.0 / MEMBERS) - total[m] * norm)
            grad_ref[m, rows, :] = g
            fsum = fsum + g
        sums.append(fsum)
    extra_ref[...] = jnp.zeros((EXTRA, LANES), F32)
    bias = jnp.sum(jnp.transpose(jnp.concatenate(sums, 0)), 0, keepdims=True)
    extra_ref[0:1, 0:VARS] = bias
    extra_ref[1:2, :] = jnp.sum(loss, 0, keepdims=True)
    extra_ref[2:3, :] = area


def weight_kernel(c_ref, g_ref, x_ref, e_ref, own_ref, other_ref):
    acc = jnp.zeros((VARS, LATENT), F32)
    for i in range(x_ref.shape[0] // BLOCK):
        rows = slice(i * BLOCK, (i + 1) * BLOCK)
        g = jnp.concatenate([g_ref[i * CHUNKS + j] for j in range(CHUNKS)], 1)
        gh, gl = split(g)
        xh, xl = split(x_ref[rows, :])
        both = dot(jnp.concatenate([gh, gl], 0), xh, (1, 0))
        acc = acc + (both[:VARS] + both[VARS:] + dot(gh, xl, (1, 0)))
    first = c_ref[0] == 0
    for i in range(HALF // LANES):
        rows = slice(i * VARS, (i + 1) * VARS)
        low = acc[:, i * LANES : (i + 1) * LANES]
        high = acc[:, HALF + i * LANES : HALF + (i + 1) * LANES]
        own_ref[rows, :] = jnp.where(first, low, high)
        other_ref[rows, :] = jnp.where(first, high, low)
    own_ref[ROWS:, :] = e_ref[...]
    other_ref[ROWS:, :] = e_ref[...]


def pair_kernel(a_ref, b_ref, out_ref):
    s = a_ref[...] + b_ref[...]
    for i in range(out_ref.shape[0]):
        out_ref[i] = s


def fold_kernel(in_ref, out_ref):
    s = in_ref[0]
    for i in range(1, in_ref.shape[0]):
        s = s + in_ref[i]
    for i in range(out_ref.shape[0]):
        out_ref[i] = s


def last_kernel(in_ref, w_ref, loss_ref, bias_ref, inv_ref):
    s = in_ref[0]
    for i in range(1, in_ref.shape[0]):
        s = s + in_ref[i]
    e = s[ROWS:]
    area = jnp.sum(e[2:3], 1, keepdims=True)
    w_ref[...] = s[:ROWS] / area
    loss_ref[...] = jnp.sum(e[1:2], 1, keepdims=True) / area
    bias_ref[...] = (e[0:1] / area)[:, :VARS]
    inv_ref[...] = jnp.broadcast_to(1.0 / area, (1, LANES))


def latent_kernel(nodes, g_ref, w_ref, inv_ref, out_hbm, out_ref, sems):
    inv = inv_ref[...] * float(nodes)
    wh, wl = split(w_ref[...])
    w = jnp.concatenate([wh, wh, wl], 0)
    copies = []
    for i in range(out_ref.shape[0] // BLOCK):
        rows = pl.ds(i * BLOCK, BLOCK)
        g = jnp.concatenate([g_ref[i * CHUNKS + j] * inv for j in range(CHUNKS)], 1)
        gh, gl = split(g)
        out_ref[rows, :] = dot(jnp.concatenate([gh, gl, gh], 0), w, (0, 0))
        copies.append(pltpu.make_async_copy(out_ref.at[rows], out_hbm.at[rows], sems.at[i]))
        copies[-1].start()
    for copy in copies:
        copy.wait()


def join_kernel(c_ref, mine_ref, theirs_ref, out_ref):
    first = c_ref[0] == 0
    for i in range(HALF // LANES):
        rows = slice(i * VARS, (i + 1) * VARS)
        mine, theirs = mine_ref[rows, :], theirs_ref[rows, :]
        out_ref[:, i * LANES : (i + 1) * LANES] = jnp.where(first, mine, theirs)
        out_ref[:, HALF + i * LANES : HALF + (i + 1) * LANES] = jnp.where(first, theirs, mine)


def whole(shape):
    return pl.BlockSpec(shape, lambda *_: (0,) * len(shape))


def shape(*s):
    return jax.ShapeDtypeStruct(s, F32)


def body(latent, dec_weight, dec_bias, target, area, var_weight):
    slab = area.shape[0]
    nodes = slab * lax.axis_size("y") * lax.axis_size("zh")
    steps = slab // BLOCK
    x = latent.reshape(slab, LATENT)
    wt = dec_weight.T
    me = lax.axis_index(MEMBER).astype(jnp.int32).reshape(1)
    core = lax.axis_index("c").astype(jnp.int32).reshape(1)

    fields, kept = pl.pallas_call(
        decode_kernel,
        out_shape=(shape(MEMBERS, VARS, LANES), shape(slab, LATENT)),
        in_specs=[SMEM, SMEM, HBM, HBM, HBM],
        out_specs=(VMEM, VMEM),
        scratch_shapes=[
            pltpu.VMEM((VARS, LATENT), F32),
            pltpu.VMEM((1, VARS), F32),
            pltpu.SemaphoreType.DMA((steps,)),
            pltpu.SemaphoreType.DMA((2,)),
        ],
        compiler_params=params(24),
    )(me, core, in_hbm(x), in_hbm(wt), in_hbm(dec_bias.reshape(1, VARS)))

    fields = lax.all_to_all(fields, MEMBER, 0, 0)

    grads, extra = pl.pallas_call(
        crps_kernel,
        out_shape=(shape(MEMBERS, VARS, LANES), shape(EXTRA, LANES)),
        grid_spec=pltpu.PrefetchScalarGridSpec(
            num_scalar_prefetch=1,
            grid=(1,),
            in_specs=[
                whole((MEMBERS, VARS, LANES)),
                pl.BlockSpec((VARS, LANES), lambda i, at: (0, at[0])),
                whole((slab // LANES, LANES)),
                whole((1, VARS)),
            ],
            out_specs=(whole((MEMBERS, VARS, LANES)), whole((EXTRA, LANES))),
        ),
        compiler_params=params(16),
    )(me, fields, target, area.reshape(slab // LANES, LANES), var_weight.reshape(1, VARS))

    grads = lax.all_to_all(grads, MEMBER, 0, 0)

    own, other = pl.pallas_call(
        weight_kernel,
        out_shape=(shape(ROWS + EXTRA, LANES),) * 2,
        in_specs=[SMEM, VMEM, VMEM, VMEM],
        out_specs=(VMEM, VMEM),
        compiler_params=params(24),
    )(core, grads, kept, extra)

    swap = [(0, 1), (1, 0)]
    came = lax.ppermute(other, "c", swap)
    plane = lax.axis_size("x") * lax.axis_size("y")
    depth = lax.axis_size("zl") * lax.axis_size("zh")
    parts = pl.pallas_call(
        pair_kernel, out_shape=shape(plane, ROWS + EXTRA, LANES), compiler_params=params(16)
    )(own, came)
    parts = lax.all_to_all(parts, ("x", "y"), 0, 0)
    parts = pl.pallas_call(
        fold_kernel, out_shape=shape(depth, ROWS + EXTRA, LANES), compiler_params=params(16)
    )(parts)
    parts = lax.all_to_all(parts, ("zl", "zh"), 0, 0)
    mine, loss, bias, inv = pl.pallas_call(
        last_kernel,
        out_shape=(shape(ROWS, LANES), shape(1, 1), shape(1, VARS), shape(1, LANES)),
        compiler_params=params(16),
    )(parts)
    theirs = lax.ppermute(mine, "c", swap)

    grad_latent = pl.pallas_call(
        lambda *refs: latent_kernel(nodes, *refs),
        out_shape=shape(slab, LATENT),
        in_specs=[VMEM, VMEM, VMEM],
        out_specs=HBM,
        scratch_shapes=[pltpu.VMEM((slab, LATENT), F32), pltpu.SemaphoreType.DMA((steps,))],
        compiler_params=params(24),
        cost_estimate=pl.CostEstimate(flops=6 * slab * VARS * LATENT, bytes_accessed=4 * slab * LATENT, transcendentals=0),
    )(grads, wt, inv)

    weight = pl.pallas_call(
        join_kernel,
        out_shape=shape(VARS, LATENT),
        in_specs=[SMEM, VMEM, VMEM],
        out_specs=VMEM,
        compiler_params=params(16),
    )(core, mine, theirs)
    return loss.reshape(()), grad_latent[None], weight.T, bias.reshape(VARS)


def solution(mesh):
    shaped = Mesh(mesh.devices.reshape(2, 4, 2, 4, 4), MEMBER + GRID)
    return jax.shard_map(
        body,
        mesh=shaped,
        in_specs=(P(MEMBER, GRID, None), P(), P(), P(None, GRID), P(GRID), P()),
        out_specs=(P(), P(MEMBER, GRID, None), P(), P()),
        check_vma=False,
    )
```

```python
import functools
import itertools

import jax
import jax.numpy as jnp
from jax import lax
from jax.experimental import pallas as pl
from jax.experimental.pallas import tpu as pltpu
from jax.sharding import Mesh, PartitionSpec as P

MEMBERS = 16
LATENT = 512
VARS = 32
SMOOTHING = 0.1
LANES = 128
BLOCK = 512
CHUNKS = BLOCK // LANES
HALF = LATENT // 2
ROWS = VARS * HALF // LANES
EXTRA = 8
SUMS = ROWS + EXTRA
MEMBER = ("zl", "x", "c")
GRID = ("y", "zh")
F32 = jnp.float32
BF16 = jnp.bfloat16
VMEM = pl.BlockSpec(memory_space=pltpu.VMEM)
SMEM = pl.BlockSpec(memory_space=pltpu.SMEM)
HBM = pl.BlockSpec(memory_space=pltpu.HBM)


def in_hbm(a):
    return pltpu.with_memory_space_constraint(a, pltpu.HBM)


def params(mib):
    return pltpu.CompilerParams(vmem_limit_bytes=mib * 1024 * 1024)


def split(a):
    hi = a.astype(BF16)
    return hi, (a - hi.astype(F32)).astype(BF16)


def dot(a, b, over):
    return lax.dot_general(a, b, (((over[0],), (over[1],)), ((), ())), preferred_element_type=F32)


def columns(row):
    return jnp.transpose(jnp.broadcast_to(row, (LANES, VARS)))


def decode_kernel(me_ref, core_ref, x_hbm, w_hbm, b_hbm, out_ref, keep_ref, send_ref, w_ref, b_ref, sems, more):
    first = [
        pltpu.make_async_copy(w_hbm, w_ref, more.at[0]),
        pltpu.make_async_copy(b_hbm, b_ref, more.at[1]),
    ]
    for copy in first:
        copy.start()
    core = core_ref[0]
    half = keep_ref.shape[0]
    jobs = []
    for part, (to_ref, side) in enumerate(((send_ref, 1 - core), (keep_ref, core))):
        for i in range(half // BLOCK):
            rows = pl.ds(i * BLOCK, BLOCK)
            source = pl.ds(pl.multiple_of(side * half, BLOCK) + i * BLOCK, BLOCK)
            copy = pltpu.make_async_copy(x_hbm.at[source], to_ref.at[rows], sems.at[part * (half // BLOCK) + i])
            copy.start()
            jobs.append((copy, to_ref, side, i))
    for copy in first:
        copy.wait()
    wh, wl = split(w_ref[...])
    both = jnp.concatenate([wh, wl], 0)
    bias = columns(b_ref[...])
    for copy, to_ref, side, i in jobs:
        copy.wait()
        xh, xl = split(to_ref[i * BLOCK : (i + 1) * BLOCK, :])
        f = dot(both, xh, (1, 1))
        f = f[:VARS] + f[VARS:] + dot(wh, xl, (1, 1))
        for j in range(CHUNKS):
            out_ref[2 * (i * CHUNKS + j) + side] = f[:, j * LANES : (j + 1) * LANES] + bias


def crps_kernel(at_ref, f_ref, t_ref, a_ref, v_ref, grad_ref, extra_ref):
    area = a_ref[pl.ds(at_ref[0], 1), :]
    scale = columns(v_ref[...]) * area
    sums = []
    loss = jnp.zeros((8, LANES), F32)
    for r in range(0, VARS, 8):
        rows = slice(r, r + 8)
        t = t_ref[rows, :]
        f = [f_ref[m, rows, :] for m in range(MEMBERS)]
        slope = [None] * MEMBERS
        near = jnp.zeros((8, LANES), F32)
        pairs = jnp.zeros((8, LANES), F32)
        total = [jnp.zeros((8, LANES), F32) for _ in range(MEMBERS)]
        for i in range(MEMBERS):
            d = f[i] - t
            q = d * d + SMOOTHING * SMOOTHING
            inv = lax.rsqrt(q)
            near = near + q * inv
            slope[i] = d * inv
            for j in range(i + 1, MEMBERS):
                d = f[i] - f[j]
                q = d * d + SMOOTHING * SMOOTHING
                inv = lax.rsqrt(q)
                pairs = pairs + q * inv
                s = d * inv
                total[i] = total[i] + s
                total[j] = total[j] - s
        norm = 1.0 / (MEMBERS * (MEMBERS - 1))
        here = scale[rows]
        loss = loss + here * (near * (1.0 / MEMBERS) - pairs * norm)
        fsum = jnp.zeros((8, LANES), F32)
        for m in range(MEMBERS):
            g = here * (slope[m] * (1.0 / MEMBERS) - total[m] * norm)
            grad_ref[m, rows, :] = g
            fsum = fsum + g
        sums.append(fsum)
    extra_ref[...] = jnp.zeros((EXTRA, LANES), F32)
    bias = jnp.sum(jnp.transpose(jnp.concatenate(sums, 0)), 0, keepdims=True)
    extra_ref[0:1, 0:VARS] = bias
    extra_ref[1:2, :] = jnp.sum(loss, 0, keepdims=True)
    extra_ref[2:3, :] = jnp.sum(a_ref[...], 0, keepdims=True)


def weight_columns(core, side, g_ref, keep_ref, got_ref, e_ref, out_ref):
    columns = pl.ds(pl.multiple_of(side * HALF, HALF), HALF)
    acc = jnp.zeros((VARS, HALF), F32)
    for x_ref, whose in ((keep_ref, core), (got_ref, 1 - core)):
        for i in range(x_ref.shape[0] // BLOCK):
            g = jnp.concatenate([g_ref[i * CHUNKS + j, whose] for j in range(CHUNKS)], 1)
            gh, gl = split(g)
            xh, xl = split(x_ref[i * BLOCK : (i + 1) * BLOCK, columns])
            both = dot(jnp.concatenate([gh, gl], 0), xh, (1, 0))
            acc = acc + (both[:VARS] + both[VARS:] + dot(gh, xl, (1, 0)))
    for i in range(HALF // LANES):
        out_ref[i * VARS : (i + 1) * VARS, :] = acc[:, i * LANES : (i + 1) * LANES]
    out_ref[ROWS:SUMS, :] = e_ref[...]


def weight_other_kernel(c_ref, g_ref, keep_ref, got_ref, e_ref, out_ref):
    core = c_ref[0]
    weight_columns(core, 1 - core, g_ref, keep_ref, got_ref, e_ref, out_ref)
    for i in range(g_ref.shape[0]):
        out_ref[SUMS + i * VARS : SUMS + (i + 1) * VARS, :] = g_ref[i, 1 - core]


def weight_own_kernel(c_ref, g_ref, keep_ref, got_ref, e_ref, out_ref):
    weight_columns(c_ref[0], c_ref[0], g_ref, keep_ref, got_ref, e_ref, out_ref)


def pair_kernel(a_ref, b_ref, *refs):
    out_ref = refs[-1]
    out_ref[...] = a_ref[...] + b_ref[:SUMS, :]


def quad_kernel(a_ref, b_ref, c_ref, d_ref, out_ref):
    out_ref[...] = (a_ref[...] + b_ref[...]) + (c_ref[...] + d_ref[...])


def latent_kernel(nodes, c_ref, g_ref, got_ref, w_ref, e_ref, out_hbm, out_ref, sems):
    core = c_ref[0]
    inv = float(nodes * MEMBERS // 2) / jnp.sum(e_ref[ROWS + 2 : ROWS + 3, :], 1, keepdims=True)
    wh, wl = split(w_ref[...])
    w = jnp.concatenate([wh, wh, wl], 0)
    half = out_ref.shape[0] // 2
    copies = []
    for part, side in enumerate((core, 1 - core)):
        for i in range(half // BLOCK):
            chips = range(i * CHUNKS, (i + 1) * CHUNKS)
            if part == 0:
                g = [g_ref[k, core] for k in chips]
            else:
                g = [got_ref[SUMS + k * VARS : SUMS + (k + 1) * VARS, :] for k in chips]
            gh, gl = split(jnp.concatenate([a * inv for a in g], 1))
            rows = pl.ds(part * half + i * BLOCK, BLOCK)
            out_ref[rows, :] = dot(jnp.concatenate([gh, gl, gh], 0), w, (0, 0))
            to = pl.ds(pl.multiple_of(side * half, BLOCK) + i * BLOCK, BLOCK)
            copies.append(pltpu.make_async_copy(out_ref.at[rows], out_hbm.at[to], sems.at[len(copies)]))
            copies[-1].start()
    for copy in copies:
        copy.wait()


def join_kernel(c_ref, a_ref, near_ref, theirs_ref, across_ref, out_ref, loss_ref, bias_ref):
    first = c_ref[0] == 0
    extra = a_ref[ROWS:, :] + near_ref[ROWS:, :]
    inv = float(MEMBERS) / jnp.sum(extra[2:3], 1, keepdims=True)
    for i in range(HALF // LANES):
        rows = slice(i * VARS, (i + 1) * VARS)
        mine = (a_ref[rows, :] + near_ref[rows, :]) * inv
        theirs = (theirs_ref[rows, :] + across_ref[rows, :]) * inv
        out_ref[:, i * LANES : (i + 1) * LANES] = jnp.where(first, mine, theirs)
        out_ref[:, HALF + i * LANES : HALF + (i + 1) * LANES] = jnp.where(first, theirs, mine)
    bias_ref[...] = extra[0:1, :VARS] * inv
    loss_ref[...] = jnp.sum(extra[1:2], 1, keepdims=True) * inv


NEAR = {0: 1, 1: 0, 2: 3, 3: 2}
FAR = {0: 3, 3: 0, 1: 2, 2: 1}
PAIRINGS = {"c": (2, {0: 1, 1: 0}), "x1": (1, NEAR), "x2": (1, FAR), "y1": (3, NEAR), "y2": (3, FAR), "z1": (4, NEAR), "z2": (4, FAR), "zl": (0, {0: 1, 1: 0})}


def trade(a, names):
    sizes = [lax.axis_size(axis) for axis in MEMBER + GRID]
    places = list(itertools.product(*[range(n) for n in sizes]))
    number = {place: i for i, place in enumerate(places)}
    pairs = []
    for place in places:
        to = list(place)
        for name in names:
            axis, pairing = PAIRINGS[name]
            to[axis] = pairing[to[axis]]
        pairs.append((number[place], number[tuple(to)]))
    return lax.ppermute(a, MEMBER + GRID, pairs)


def add_round(a, names, *after):
    if len(names) == 1:
        others = [trade(a, names)]
        kernel = pair_kernel
    else:
        others = [trade(a, names[:1]), trade(a, names[1:]), trade(a, names)]
        kernel = quad_kernel
    return pl.pallas_call(kernel, out_shape=shape(SUMS, LANES), compiler_params=params(16))(a, *others, *after)


def whole(shape):
    return pl.BlockSpec(shape, lambda *_: (0,) * len(shape))


def shape(*s):
    return jax.ShapeDtypeStruct(s, F32)


def body(latent, dec_weight, dec_bias, target, area, var_weight):
    slab = area.shape[0]
    nodes = slab * lax.axis_size("y") * lax.axis_size("zh")
    steps = slab // BLOCK
    half = slab // 2
    chips = MEMBERS // 2
    x = latent.reshape(slab, LATENT)
    wt = dec_weight.T
    core = lax.axis_index("c").astype(jnp.int32).reshape(1)
    at = core * chips + lax.axis_index(("zl", "x")).astype(jnp.int32).reshape(1)
    swap = [(0, 1), (1, 0)]

    fields, keep, send = pl.pallas_call(
        decode_kernel,
        out_shape=(shape(MEMBERS, VARS, LANES), shape(half, LATENT), shape(half, LATENT)),
        in_specs=[SMEM, SMEM, HBM, HBM, HBM],
        out_specs=(VMEM, VMEM, VMEM),
        scratch_shapes=[
            pltpu.VMEM((VARS, LATENT), F32),
            pltpu.VMEM((1, VARS), F32),
            pltpu.SemaphoreType.DMA((steps,)),
            pltpu.SemaphoreType.DMA((2,)),
        ],
        compiler_params=params(24),
    )(at, core, in_hbm(x), in_hbm(wt), in_hbm(dec_bias.reshape(1, VARS)))

    got = lax.ppermute(send, "c", swap)
    fields = lax.all_to_all(fields, MEMBER, 0, 0)

    grads, extra = pl.pallas_call(
        crps_kernel,
        out_shape=(shape(MEMBERS, VARS, LANES), shape(EXTRA, LANES)),
        grid_spec=pltpu.PrefetchScalarGridSpec(
            num_scalar_prefetch=1,
            grid=(1,),
            in_specs=[
                whole((MEMBERS, VARS, LANES)),
                pl.BlockSpec((VARS, LANES), lambda i, at: (0, at[0])),
                whole((slab // LANES, LANES)),
                whole((1, VARS)),
            ],
            out_specs=(whole((MEMBERS, VARS, LANES)), whole((EXTRA, LANES))),
        ),
        compiler_params=params(16),
    )(at, fields, target, area.reshape(slab // LANES, LANES), var_weight.reshape(1, VARS))

    grads = lax.all_to_all(grads.reshape(chips, 2, VARS, LANES), ("zl", "x"), 0, 0)

    def weight(kernel, rows):
        return pl.pallas_call(
            kernel,
            out_shape=shape(rows, LANES),
            in_specs=[SMEM, VMEM, VMEM, VMEM, VMEM],
            out_specs=VMEM,
            compiler_params=params(24),
            cost_estimate=pl.CostEstimate(flops=6 * slab * VARS * HALF, bytes_accessed=4 * slab * HALF, transcendentals=0),
        )(core, grads, keep, got, extra)

    other = weight(weight_other_kernel, SUMS + chips * VARS)
    came = lax.ppermute(other, "c", swap)
    own = weight(weight_own_kernel, SUMS)
    sums = pl.pallas_call(pair_kernel, out_shape=shape(SUMS, LANES), compiler_params=params(16))(own, came)
    sums = add_round(sums, ("x1", "y1"))
    sums = add_round(sums, ("x2", "y2"))
    sums = add_round(sums, ("z2",))
    sums = add_round(sums, ("z1",))
    across = trade(sums, ("zl", "c"))
    near = trade(sums, ("zl",))
    theirs = trade(sums, ("c",))

    grad_latent = pl.pallas_call(
        lambda *refs: latent_kernel(nodes, *refs),
        out_shape=shape(slab, LATENT),
        in_specs=[SMEM, VMEM, VMEM, VMEM, VMEM],
        out_specs=HBM,
        scratch_shapes=[pltpu.VMEM((slab, LATENT), F32), pltpu.SemaphoreType.DMA((steps,))],
        compiler_params=params(24),
        cost_estimate=pl.CostEstimate(flops=6 * slab * VARS * LATENT, bytes_accessed=4 * slab * LATENT, transcendentals=0),
    )(core, grads, came, wt, sums)

    grad_weight, loss, bias = pl.pallas_call(
        join_kernel,
        out_shape=(shape(VARS, LATENT), shape(1, 1), shape(1, VARS)),
        in_specs=[SMEM, VMEM, VMEM, VMEM, VMEM],
        out_specs=(VMEM, VMEM, VMEM),
        compiler_params=params(16),
    )(core, sums, near, theirs, across)
    return loss.reshape(()), grad_latent[None], grad_weight.T, bias.reshape(VARS)


def solution(mesh):
    shaped = Mesh(mesh.devices.reshape(2, 4, 2, 4, 4), MEMBER + GRID)
    return jax.shard_map(
        body,
        mesh=shaped,
        in_specs=(P(MEMBER, GRID, None), P(), P(), P(None, GRID), P(GRID), P()),
        out_specs=(P(), P(MEMBER, GRID, None), P(), P()),
        check_vma=False,
    )
```

```python
import functools
import itertools

import jax
import jax.numpy as jnp
from jax import lax
from jax.experimental import pallas as pl
from jax.experimental.pallas import tpu as pltpu
from jax.sharding import Mesh, PartitionSpec as P

MEMBERS = 16
LATENT = 512
VARS = 32
SMOOTHING = 0.1
LANES = 128
BLOCK = 512
CHUNKS = BLOCK // LANES
HALF = LATENT // 2
ROWS = VARS * HALF // LANES
EXTRA = 8
SUMS = ROWS + EXTRA
MEMBER = ("zl", "x", "c")
GRID = ("y", "zh")
F32 = jnp.float32
BF16 = jnp.bfloat16
VMEM = pl.BlockSpec(memory_space=pltpu.VMEM)
SMEM = pl.BlockSpec(memory_space=pltpu.SMEM)
HBM = pl.BlockSpec(memory_space=pltpu.HBM)


def in_hbm(a):
    return pltpu.with_memory_space_constraint(a, pltpu.HBM)


def params(mib):
    return pltpu.CompilerParams(vmem_limit_bytes=mib * 1024 * 1024)


def split(a):
    hi = a.astype(BF16)
    return hi, (a - hi.astype(F32)).astype(BF16)


def dot(a, b, over):
    return lax.dot_general(a, b, (((over[0],), (over[1],)), ((), ())), preferred_element_type=F32)


def columns(row):
    return jnp.transpose(jnp.broadcast_to(row, (LANES, VARS)))


def decode_kernel(me_ref, held_ref, core_ref, x_hbm, w_hbm, b_hbm, out_ref, keep_ref, send_ref, w_ref, b_ref, sems, more):
    first = [
        pltpu.make_async_copy(w_hbm, w_ref, more.at[0]),
        pltpu.make_async_copy(b_hbm, b_ref, more.at[1]),
    ]
    for copy in first:
        copy.start()
    core = core_ref[0]
    half = keep_ref.shape[0]
    jobs = []
    for part, (to_ref, side) in enumerate(((send_ref, 1 - core), (keep_ref, core))):
        source = pl.ds(pl.multiple_of(side * half, BLOCK), half)
        copy = pltpu.make_async_copy(x_hbm.at[source], to_ref, sems.at[part])
        copy.start()
        jobs.append((copy, to_ref, side))
    for copy in first:
        copy.wait()
    wh, wl = split(w_ref[...])
    both = jnp.concatenate([wh, wl], 0)
    bias = columns(b_ref[...])
    for copy, to_ref, side in jobs:
        copy.wait()
        xh, xl = split(to_ref[...])
        f = dot(both, xh, (1, 1))
        f = f[:VARS] + f[VARS:] + dot(wh, xl, (1, 1))
        for j in range(half // LANES):
            out_ref[2 * j + side] = f[:, j * LANES : (j + 1) * LANES] + bias


def crps_kernel(at_ref, f_ref, t_ref, a_ref, v_ref, grad_ref, extra_ref):
    area = a_ref[pl.ds(at_ref[0], 1), :]
    scale = columns(v_ref[...]) * area
    sums = []
    loss = jnp.zeros((8, LANES), F32)
    for r in range(0, VARS, 8):
        rows = slice(r, r + 8)
        t = t_ref[rows, :]
        f = [f_ref[m, rows, :] for m in range(MEMBERS)]
        slope = [None] * MEMBERS
        near = jnp.zeros((8, LANES), F32)
        pairs = jnp.zeros((8, LANES), F32)
        total = [jnp.zeros((8, LANES), F32) for _ in range(MEMBERS)]
        for i in range(MEMBERS):
            d = f[i] - t
            q = d * d + SMOOTHING * SMOOTHING
            inv = lax.rsqrt(q)
            near = near + q * inv
            slope[i] = d * inv
            for j in range(i + 1, MEMBERS):
                d = f[i] - f[j]
                q = d * d + SMOOTHING * SMOOTHING
                inv = lax.rsqrt(q)
                pairs = pairs + q * inv
                s = d * inv
                total[i] = total[i] + s
                total[j] = total[j] - s
        norm = 1.0 / (MEMBERS * (MEMBERS - 1))
        here = scale[rows]
        loss = loss + here * (near * (1.0 / MEMBERS) - pairs * norm)
        fsum = jnp.zeros((8, LANES), F32)
        for m in range(MEMBERS):
            g = here * (slope[m] * (1.0 / MEMBERS) - total[m] * norm)
            grad_ref[m, rows, :] = g
            fsum = fsum + g
        sums.append(fsum)
    extra_ref[...] = jnp.zeros((EXTRA, LANES), F32)
    bias = jnp.sum(jnp.transpose(jnp.concatenate(sums, 0)), 0, keepdims=True)
    extra_ref[0:1, 0:VARS] = bias
    extra_ref[1:2, :] = jnp.sum(loss, 0, keepdims=True)
    extra_ref[2:3, :] = jnp.sum(a_ref[...], 0, keepdims=True)


def weight_columns(core, side, g_ref, keep_ref, got_ref, e_ref, out_ref):
    columns = pl.ds(pl.multiple_of(side * HALF, HALF), HALF)
    acc = jnp.zeros((VARS, HALF), F32)
    for x_ref, whose in ((keep_ref, core), (got_ref, 1 - core)):
        for i in range(x_ref.shape[0] // BLOCK):
            g = jnp.concatenate([g_ref[i * CHUNKS + j, whose] for j in range(CHUNKS)], 1)
            gh, gl = split(g)
            xh, xl = split(x_ref[i * BLOCK : (i + 1) * BLOCK, columns])
            both = dot(jnp.concatenate([gh, gl], 0), xh, (1, 0))
            acc = acc + (both[:VARS] + both[VARS:] + dot(gh, xl, (1, 0)))
    for i in range(HALF // LANES):
        out_ref[i * VARS : (i + 1) * VARS, :] = acc[:, i * LANES : (i + 1) * LANES]
    out_ref[ROWS:SUMS, :] = e_ref[...]


def weight_other_kernel(c_ref, h_ref, g_ref, keep_ref, got_ref, e_ref, out_ref):
    core = c_ref[0]
    weight_columns(core, 1 - h_ref[0], g_ref, keep_ref, got_ref, e_ref, out_ref)
    for i in range(g_ref.shape[0]):
        out_ref[SUMS + i * VARS : SUMS + (i + 1) * VARS, :] = g_ref[i, 1 - core]


def weight_own_kernel(c_ref, h_ref, g_ref, keep_ref, got_ref, e_ref, out_ref):
    weight_columns(c_ref[0], h_ref[0], g_ref, keep_ref, got_ref, e_ref, out_ref)


def pair_kernel(a_ref, b_ref, *refs):
    out_ref = refs[-1]
    out_ref[...] = a_ref[...] + b_ref[:SUMS, :]


def quad_kernel(a_ref, b_ref, c_ref, d_ref, out_ref):
    out_ref[...] = (a_ref[...] + b_ref[...]) + (c_ref[...] + d_ref[...])


def latent_kernel(nodes, c_ref, g_ref, got_ref, w_ref, e_ref, out_hbm, out_ref, sems):
    core = c_ref[0]
    inv = float(nodes * MEMBERS) / jnp.sum(e_ref[ROWS + 2 : ROWS + 3, :], 1, keepdims=True)
    wh, wl = split(w_ref[...])
    w = jnp.concatenate([wh, wh, wl], 0)
    half = out_ref.shape[0] // 2
    copies = []
    for part, side in enumerate((core, 1 - core)):
        for i in range(half // BLOCK):
            chips = range(i * CHUNKS, (i + 1) * CHUNKS)
            if part == 0:
                g = [g_ref[k, core] for k in chips]
            else:
                g = [got_ref[SUMS + k * VARS : SUMS + (k + 1) * VARS, :] for k in chips]
            gh, gl = split(jnp.concatenate([a * inv for a in g], 1))
            rows = pl.ds(part * half + i * BLOCK, BLOCK)
            out_ref[rows, :] = dot(jnp.concatenate([gh, gl, gh], 0), w, (0, 0))
            to = pl.ds(pl.multiple_of(side * half, BLOCK) + i * BLOCK, BLOCK)
            copies.append(pltpu.make_async_copy(out_ref.at[rows], out_hbm.at[to], sems.at[len(copies)]))
            copies[-1].start()
    for copy in copies:
        copy.wait()


def join_kernel(c_ref, mine_ref, theirs_ref, out_ref, loss_ref, bias_ref):
    first = c_ref[0] == 0
    extra = mine_ref[ROWS:, :]
    inv = float(MEMBERS) / jnp.sum(extra[2:3], 1, keepdims=True)
    for i in range(HALF // LANES):
        rows = slice(i * VARS, (i + 1) * VARS)
        mine, theirs = mine_ref[rows, :] * inv, theirs_ref[rows, :] * inv
        out_ref[:, i * LANES : (i + 1) * LANES] = jnp.where(first, mine, theirs)
        out_ref[:, HALF + i * LANES : HALF + (i + 1) * LANES] = jnp.where(first, theirs, mine)
    bias_ref[...] = extra[0:1, :VARS] * inv
    loss_ref[...] = jnp.sum(extra[1:2], 1, keepdims=True) * inv


NEAR = {0: 1, 1: 0, 2: 3, 3: 2}
FAR = {0: 3, 3: 0, 1: 2, 2: 1}
PAIRINGS = {"x1": (1, NEAR), "x2": (1, FAR), "y1": (3, NEAR), "y2": (3, FAR), "z1": (4, NEAR), "z2": (4, FAR), "zl": (0, {0: 1, 1: 0})}


def trade(a, names):
    sizes = [lax.axis_size(axis) for axis in MEMBER + GRID]
    places = list(itertools.product(*[range(n) for n in sizes]))
    number = {place: i for i, place in enumerate(places)}
    pairs = []
    for place in places:
        to = list(place)
        for name in names:
            axis, pairing = PAIRINGS[name]
            to[axis] = pairing[to[axis]]
            to[2] = 1 - to[2]
        pairs.append((number[place], number[tuple(to)]))
    return lax.ppermute(a, MEMBER + GRID, pairs)


def add_round(a, names, *after):
    if len(names) == 1:
        others = [trade(a, names)]
        kernel = pair_kernel
    else:
        others = [trade(a, names[:1]), trade(a, names[1:]), trade(a, names)]
        kernel = quad_kernel
    return pl.pallas_call(kernel, out_shape=shape(SUMS, LANES), compiler_params=params(16))(a, *others, *after)


def whole(shape):
    return pl.BlockSpec(shape, lambda *_: (0,) * len(shape))


def shape(*s):
    return jax.ShapeDtypeStruct(s, F32)


def body(latent, dec_weight, dec_bias, target, area, var_weight):
    slab = area.shape[0]
    nodes = slab * lax.axis_size("y") * lax.axis_size("zh")
    steps = slab // BLOCK
    half = slab // 2
    chips = MEMBERS // 2
    x = latent.reshape(slab, LATENT)
    wt = dec_weight.T
    core = lax.axis_index("c").astype(jnp.int32).reshape(1)
    at = core * chips + lax.axis_index(("zl", "x")).astype(jnp.int32).reshape(1)
    held = (core + sum(lax.axis_index(axis) for axis in ("zl", "x", "y", "zh"))).astype(jnp.int32) & 1
    swap = [(0, 1), (1, 0)]

    fields, keep, send = pl.pallas_call(
        decode_kernel,
        out_shape=(shape(MEMBERS, VARS, LANES), shape(half, LATENT), shape(half, LATENT)),
        in_specs=[SMEM, SMEM, SMEM, HBM, HBM, HBM],
        out_specs=(VMEM, VMEM, VMEM),
        scratch_shapes=[
            pltpu.VMEM((VARS, LATENT), F32),
            pltpu.VMEM((1, VARS), F32),
            pltpu.SemaphoreType.DMA((2,)),
            pltpu.SemaphoreType.DMA((2,)),
        ],
        compiler_params=params(24),
    )(at, held, core, in_hbm(x), in_hbm(wt), in_hbm(dec_bias.reshape(1, VARS)))

    got = lax.ppermute(send, "c", swap)
    fields = lax.all_to_all(fields, MEMBER, 0, 0)

    grads, extra = pl.pallas_call(
        crps_kernel,
        out_shape=(shape(MEMBERS, VARS, LANES), shape(EXTRA, LANES)),
        grid_spec=pltpu.PrefetchScalarGridSpec(
            num_scalar_prefetch=1,
            grid=(1,),
            in_specs=[
                whole((MEMBERS, VARS, LANES)),
                pl.BlockSpec((VARS, LANES), lambda i, at: (0, at[0])),
                whole((slab // LANES, LANES)),
                whole((1, VARS)),
            ],
            out_specs=(whole((MEMBERS, VARS, LANES)), whole((EXTRA, LANES))),
        ),
        compiler_params=params(16),
    )(at, fields, target, area.reshape(slab // LANES, LANES), var_weight.reshape(1, VARS))

    grads = lax.all_to_all(grads.reshape(chips, 2, VARS, LANES), ("zl", "x"), 0, 0)

    def weight(kernel, rows):
        return pl.pallas_call(
            kernel,
            out_shape=shape(rows, LANES),
            in_specs=[SMEM, SMEM, VMEM, VMEM, VMEM, VMEM],
            out_specs=VMEM,
            compiler_params=params(24),
            cost_estimate=pl.CostEstimate(flops=6 * slab * VARS * HALF, bytes_accessed=4 * slab * HALF, transcendentals=0),
        )(core, held, grads, keep, got, extra)

    other = weight(weight_other_kernel, SUMS + chips * VARS)
    came = lax.ppermute(other, "c", swap)
    own = weight(weight_own_kernel, SUMS)
    sums = pl.pallas_call(pair_kernel, out_shape=shape(SUMS, LANES), compiler_params=params(16))(own, came)
    sums = add_round(sums, ("x1", "y1"))
    sums = add_round(sums, ("x2", "y2"))
    sums = add_round(sums, ("zl", "z1"))
    sums = add_round(sums, ("z2",))
    theirs = lax.ppermute(sums, "c", swap)

    grad_latent = pl.pallas_call(
        lambda *refs: latent_kernel(nodes, *refs),
        out_shape=shape(slab, LATENT),
        in_specs=[SMEM, VMEM, VMEM, VMEM, VMEM],
        out_specs=HBM,
        scratch_shapes=[pltpu.VMEM((slab, LATENT), F32), pltpu.SemaphoreType.DMA((steps,))],
        compiler_params=params(24),
        cost_estimate=pl.CostEstimate(flops=6 * slab * VARS * LATENT, bytes_accessed=4 * slab * LATENT, transcendentals=0),
    )(core, grads, came, wt, sums)

    grad_weight, loss, bias = pl.pallas_call(
        join_kernel,
        out_shape=(shape(VARS, LATENT), shape(1, 1), shape(1, VARS)),
        in_specs=[SMEM, VMEM, VMEM],
        out_specs=(VMEM, VMEM, VMEM),
        compiler_params=params(16),
    )(held, sums, theirs)
    return loss.reshape(()), grad_latent[None], grad_weight.T, bias.reshape(VARS)


def solution(mesh):
    shaped = Mesh(mesh.devices.reshape(2, 4, 2, 4, 4), MEMBER + GRID)
    return jax.shard_map(
        body,
        mesh=shaped,
        in_specs=(P(MEMBER, GRID, None), P(), P(), P(None, GRID), P(GRID), P()),
        out_specs=(P(), P(MEMBER, GRID, None), P(), P()),
        check_vma=False,
    )
```

```python
import functools
import itertools

import jax
import jax.numpy as jnp
from jax import lax
from jax.experimental import pallas as pl
from jax.experimental.pallas import tpu as pltpu
from jax.sharding import Mesh, PartitionSpec as P

MEMBERS = 16
LATENT = 512
VARS = 32
SMOOTHING = 0.1
LANES = 128
BLOCK = 512
CHUNKS = BLOCK // LANES
HALF = LATENT // 2
ROWS = VARS * HALF // LANES
EXTRA = 8
SUMS = ROWS + EXTRA
MEMBER = ("zl", "x", "c")
GRID = ("y", "zh")
F32 = jnp.float32
BF16 = jnp.bfloat16
VMEM = pl.BlockSpec(memory_space=pltpu.VMEM)
SMEM = pl.BlockSpec(memory_space=pltpu.SMEM)
HBM = pl.BlockSpec(memory_space=pltpu.HBM)


def in_hbm(a):
    return pltpu.with_memory_space_constraint(a, pltpu.HBM)


def params(mib):
    return pltpu.CompilerParams(vmem_limit_bytes=mib * 1024 * 1024)


def split(a):
    hi = a.astype(BF16)
    return hi, (a - hi.astype(F32)).astype(BF16)


def dot(a, b, over):
    return lax.dot_general(a, b, (((over[0],), (over[1],)), ((), ())), preferred_element_type=F32)


def columns(row):
    return jnp.transpose(jnp.broadcast_to(row, (LANES, VARS)))


def decode_kernel(me_ref, held_ref, core_ref, x_hbm, w_hbm, b_hbm, out_ref, keep_ref, send_ref, w_ref, b_ref, sems, more):
    first = [
        pltpu.make_async_copy(w_hbm, w_ref, more.at[0]),
        pltpu.make_async_copy(b_hbm, b_ref, more.at[1]),
    ]
    for copy in first:
        copy.start()
    core = core_ref[0]
    half = keep_ref.shape[0]
    jobs = []
    for part, (to_ref, side) in enumerate(((send_ref, 1 - core), (keep_ref, core))):
        source = pl.ds(pl.multiple_of(side * half, BLOCK), half)
        copy = pltpu.make_async_copy(x_hbm.at[source], to_ref, sems.at[part])
        copy.start()
        jobs.append((copy, to_ref, side))
    for copy in first:
        copy.wait()
    wh, wl = split(w_ref[...])
    both = jnp.concatenate([wh, wl], 0)
    bias = columns(b_ref[...])
    for copy, to_ref, side in jobs:
        copy.wait()
        xh, xl = split(to_ref[...])
        f = dot(both, xh, (1, 1))
        f = f[:VARS] + f[VARS:] + dot(wh, xl, (1, 1))
        for j in range(half // LANES):
            out_ref[2 * j + side] = f[:, j * LANES : (j + 1) * LANES] + bias


def crps_kernel(at_ref, f_ref, t_ref, a_ref, v_ref, grad_ref, extra_ref):
    area = a_ref[pl.ds(at_ref[0], 1), :]
    scale = columns(v_ref[...]) * area
    sums = []
    loss = jnp.zeros((8, LANES), F32)
    for r in range(0, VARS, 8):
        rows = slice(r, r + 8)
        t = t_ref[rows, :]
        f = [f_ref[m, rows, :] for m in range(MEMBERS)]
        slope = [None] * MEMBERS
        near = jnp.zeros((8, LANES), F32)
        pairs = jnp.zeros((8, LANES), F32)
        total = [jnp.zeros((8, LANES), F32) for _ in range(MEMBERS)]
        for i in range(MEMBERS):
            d = f[i] - t
            q = d * d + SMOOTHING * SMOOTHING
            inv = lax.rsqrt(q)
            near = near + q * inv
            slope[i] = d * inv
            for j in range(i + 1, MEMBERS):
                d = f[i] - f[j]
                q = d * d + SMOOTHING * SMOOTHING
                inv = lax.rsqrt(q)
                pairs = pairs + q * inv
                s = d * inv
                total[i] = total[i] + s
                total[j] = total[j] - s
        norm = 1.0 / (MEMBERS * (MEMBERS - 1))
        here = scale[rows]
        loss = loss + here * (near * (1.0 / MEMBERS) - pairs * norm)
        fsum = jnp.zeros((8, LANES), F32)
        for m in range(MEMBERS):
            g = here * (slope[m] * (1.0 / MEMBERS) - total[m] * norm)
            grad_ref[m, rows, :] = g
            fsum = fsum + g
        sums.append(fsum)
    extra_ref[...] = jnp.zeros((EXTRA, LANES), F32)
    bias = jnp.sum(jnp.transpose(jnp.concatenate(sums, 0)), 0, keepdims=True)
    extra_ref[0:1, 0:VARS] = bias
    extra_ref[1:2, :] = jnp.sum(loss, 0, keepdims=True)
    extra_ref[2:3, :] = jnp.sum(a_ref[...], 0, keepdims=True)


def weight_columns(core, side, g_ref, keep_ref, got_ref, e_ref, out_ref):
    columns = pl.ds(pl.multiple_of(side * HALF, HALF), HALF)
    acc = jnp.zeros((VARS, HALF), F32)
    for x_ref, whose in ((keep_ref, core), (got_ref, 1 - core)):
        for i in range(x_ref.shape[0] // BLOCK):
            g = jnp.concatenate([g_ref[i * CHUNKS + j, whose] for j in range(CHUNKS)], 1)
            gh, gl = split(g)
            xh, xl = split(x_ref[i * BLOCK : (i + 1) * BLOCK, columns])
            both = dot(jnp.concatenate([gh, gl], 0), xh, (1, 0))
            acc = acc + (both[:VARS] + both[VARS:] + dot(gh, xl, (1, 0)))
    for i in range(HALF // LANES):
        out_ref[i * VARS : (i + 1) * VARS, :] = acc[:, i * LANES : (i + 1) * LANES]
    out_ref[ROWS:SUMS, :] = e_ref[...]


def weight_other_kernel(c_ref, h_ref, g_ref, keep_ref, got_ref, e_ref, out_ref):
    weight_columns(c_ref[0], 1 - h_ref[0], g_ref, keep_ref, got_ref, e_ref, out_ref)


def weight_own_kernel(c_ref, h_ref, g_ref, keep_ref, got_ref, e_ref, out_ref, send_ref):
    core = c_ref[0]
    weight_columns(core, h_ref[0], g_ref, keep_ref, got_ref, e_ref, out_ref)
    for i in range(g_ref.shape[0]):
        send_ref[i] = g_ref[i, 1 - core]


def pair_kernel(a_ref, b_ref, *refs):
    out_ref = refs[-1]
    out_ref[...] = a_ref[...] + b_ref[...]


def quad_kernel(a_ref, b_ref, c_ref, d_ref, out_ref):
    out_ref[...] = (a_ref[...] + b_ref[...]) + (c_ref[...] + d_ref[...])


def latent_kernel(nodes, c_ref, g_ref, got_ref, w_ref, e_ref, out_hbm, out_ref, sems):
    core = c_ref[0]
    inv = float(nodes * MEMBERS) / jnp.sum(e_ref[ROWS + 2 : ROWS + 3, :], 1, keepdims=True)
    wh, wl = split(w_ref[...])
    w = jnp.concatenate([wh, wh, wl], 0)
    half = out_ref.shape[0] // 2
    copies = []
    for part, side in enumerate((core, 1 - core)):
        for i in range(half // BLOCK):
            chips = range(i * CHUNKS, (i + 1) * CHUNKS)
            if part == 0:
                g = [g_ref[k, core] for k in chips]
            else:
                g = [got_ref[k] for k in chips]
            gh, gl = split(jnp.concatenate([a * inv for a in g], 1))
            rows = pl.ds(part * half + i * BLOCK, BLOCK)
            out_ref[rows, :] = dot(jnp.concatenate([gh, gl, gh], 0), w, (0, 0))
            to = pl.ds(pl.multiple_of(side * half, BLOCK) + i * BLOCK, BLOCK)
            copies.append(pltpu.make_async_copy(out_ref.at[rows], out_hbm.at[to], sems.at[len(copies)]))
            copies[-1].start()
    for copy in copies:
        copy.wait()


def join_kernel(c_ref, mine_ref, theirs_ref, out_ref, loss_ref, bias_ref):
    first = c_ref[0] == 0
    extra = mine_ref[ROWS:, :]
    inv = float(MEMBERS) / jnp.sum(extra[2:3], 1, keepdims=True)
    for i in range(HALF // LANES):
        rows = slice(i * VARS, (i + 1) * VARS)
        mine, theirs = mine_ref[rows, :] * inv, theirs_ref[rows, :] * inv
        out_ref[:, i * LANES : (i + 1) * LANES] = jnp.where(first, mine, theirs)
        out_ref[:, HALF + i * LANES : HALF + (i + 1) * LANES] = jnp.where(first, theirs, mine)
    bias_ref[...] = extra[0:1, :VARS] * inv
    loss_ref[...] = jnp.sum(extra[1:2], 1, keepdims=True) * inv


NEAR = {0: 1, 1: 0, 2: 3, 3: 2}
FAR = {0: 3, 3: 0, 1: 2, 2: 1}
PAIRINGS = {"x1": (1, NEAR), "x2": (1, FAR), "y1": (3, NEAR), "y2": (3, FAR), "z1": (4, NEAR), "z2": (4, FAR), "zl": (0, {0: 1, 1: 0})}


def trade(a, names):
    sizes = [lax.axis_size(axis) for axis in MEMBER + GRID]
    places = list(itertools.product(*[range(n) for n in sizes]))
    number = {place: i for i, place in enumerate(places)}
    pairs = []
    for place in places:
        to = list(place)
        for name in names:
            axis, pairing = PAIRINGS[name]
            to[axis] = pairing[to[axis]]
            to[2] = 1 - to[2]
        pairs.append((number[place], number[tuple(to)]))
    return lax.ppermute(a, MEMBER + GRID, pairs)


def add_round(a, names, *after):
    if len(names) == 1:
        others = [trade(a, names)]
        kernel = pair_kernel
    else:
        others = [trade(a, names[:1]), trade(a, names[1:]), trade(a, names)]
        kernel = quad_kernel
    return pl.pallas_call(kernel, out_shape=shape(SUMS, LANES), compiler_params=params(16))(a, *others, *after)


def whole(shape):
    return pl.BlockSpec(shape, lambda *_: (0,) * len(shape))


def shape(*s):
    return jax.ShapeDtypeStruct(s, F32)


def body(latent, dec_weight, dec_bias, target, area, var_weight):
    slab = area.shape[0]
    nodes = slab * lax.axis_size("y") * lax.axis_size("zh")
    steps = slab // BLOCK
    half = slab // 2
    chips = MEMBERS // 2
    x = latent.reshape(slab, LATENT)
    wt = dec_weight.T
    core = lax.axis_index("c").astype(jnp.int32).reshape(1)
    at = core * chips + lax.axis_index(("zl", "x")).astype(jnp.int32).reshape(1)
    held = (core + sum(lax.axis_index(axis) for axis in ("zl", "x", "y", "zh"))).astype(jnp.int32) & 1
    swap = [(0, 1), (1, 0)]

    fields, keep, send = pl.pallas_call(
        decode_kernel,
        out_shape=(shape(MEMBERS, VARS, LANES), shape(half, LATENT), shape(half, LATENT)),
        in_specs=[SMEM, SMEM, SMEM, HBM, HBM, HBM],
        out_specs=(VMEM, VMEM, VMEM),
        scratch_shapes=[
            pltpu.VMEM((VARS, LATENT), F32),
            pltpu.VMEM((1, VARS), F32),
            pltpu.SemaphoreType.DMA((2,)),
            pltpu.SemaphoreType.DMA((2,)),
        ],
        compiler_params=params(24),
    )(at, held, core, in_hbm(x), in_hbm(wt), in_hbm(dec_bias.reshape(1, VARS)))

    got = lax.ppermute(send, "c", swap)
    fields = lax.all_to_all(fields, MEMBER, 0, 0)

    grads, extra = pl.pallas_call(
        crps_kernel,
        out_shape=(shape(MEMBERS, VARS, LANES), shape(EXTRA, LANES)),
        grid_spec=pltpu.PrefetchScalarGridSpec(
            num_scalar_prefetch=1,
            grid=(1,),
            in_specs=[
                whole((MEMBERS, VARS, LANES)),
                pl.BlockSpec((VARS, LANES), lambda i, at: (0, at[0])),
                whole((slab // LANES, LANES)),
                whole((1, VARS)),
            ],
            out_specs=(whole((MEMBERS, VARS, LANES)), whole((EXTRA, LANES))),
        ),
        compiler_params=params(16),
    )(at, fields, target, area.reshape(slab // LANES, LANES), var_weight.reshape(1, VARS))

    grads = lax.all_to_all(grads.reshape(chips, 2, VARS, LANES), ("zl", "x"), 0, 0)

    def weight(kernel, *outs):
        return pl.pallas_call(
            kernel,
            out_shape=outs,
            in_specs=[SMEM, SMEM, VMEM, VMEM, VMEM, VMEM],
            out_specs=(VMEM,) * len(outs),
            compiler_params=params(24),
            cost_estimate=pl.CostEstimate(flops=6 * slab * VARS * HALF, bytes_accessed=4 * slab * HALF, transcendentals=0),
        )(core, held, grads, keep, got, extra)

    (other,) = weight(weight_other_kernel, shape(SUMS, LANES))
    came = lax.ppermute(other, "c", swap)
    own, send = weight(weight_own_kernel, shape(SUMS, LANES), shape(chips, VARS, LANES))
    rest = lax.ppermute(send, "c", swap)
    sums = pl.pallas_call(pair_kernel, out_shape=shape(SUMS, LANES), compiler_params=params(16))(own, came)
    sums = add_round(sums, ("x1", "zl"))
    sums = add_round(sums, ("x2", "y2"))
    sums = add_round(sums, ("y1", "z1"))
    sums = add_round(sums, ("z2",))
    theirs = lax.ppermute(sums, "c", swap)

    grad_latent = pl.pallas_call(
        lambda *refs: latent_kernel(nodes, *refs),
        out_shape=shape(slab, LATENT),
        in_specs=[SMEM, VMEM, VMEM, VMEM, VMEM],
        out_specs=HBM,
        scratch_shapes=[pltpu.VMEM((slab, LATENT), F32), pltpu.SemaphoreType.DMA((steps,))],
        compiler_params=params(24),
        cost_estimate=pl.CostEstimate(flops=6 * slab * VARS * LATENT, bytes_accessed=4 * slab * LATENT, transcendentals=0),
    )(core, grads, rest, wt, sums)

    grad_weight, loss, bias = pl.pallas_call(
        join_kernel,
        out_shape=(shape(VARS, LATENT), shape(1, 1), shape(1, VARS)),
        in_specs=[SMEM, VMEM, VMEM],
        out_specs=(VMEM, VMEM, VMEM),
        compiler_params=params(16),
    )(held, sums, theirs)
    return loss.reshape(()), grad_latent[None], grad_weight.T, bias.reshape(VARS)


def solution(mesh):
    shaped = Mesh(mesh.devices.reshape(2, 4, 2, 4, 4), MEMBER + GRID)
    return jax.shard_map(
        body,
        mesh=shaped,
        in_specs=(P(MEMBER, GRID, None), P(), P(), P(None, GRID), P(GRID), P()),
        out_specs=(P(), P(MEMBER, GRID, None), P(), P()),
        check_vma=False,
    )
```

```python
import functools
import itertools

import jax
import jax.numpy as jnp
from jax import lax
from jax.experimental import pallas as pl
from jax.experimental.pallas import tpu as pltpu
from jax.sharding import Mesh, PartitionSpec as P

MEMBERS = 16
LATENT = 512
VARS = 32
SMOOTHING = 0.1
LANES = 128
BLOCK = 512
CHUNKS = BLOCK // LANES
HALF = LATENT // 2
ROWS = VARS * HALF // LANES
EXTRA = 8
SUMS = ROWS + EXTRA
MEMBER = ("zl", "x", "c")
GRID = ("y", "zh")
F32 = jnp.float32
BF16 = jnp.bfloat16
VMEM = pl.BlockSpec(memory_space=pltpu.VMEM)
SMEM = pl.BlockSpec(memory_space=pltpu.SMEM)
HBM = pl.BlockSpec(memory_space=pltpu.HBM)


def in_hbm(a):
    return pltpu.with_memory_space_constraint(a, pltpu.HBM)


def params(mib):
    return pltpu.CompilerParams(vmem_limit_bytes=mib * 1024 * 1024)


def split(a):
    hi = a.astype(BF16)
    return hi, (a - hi.astype(F32)).astype(BF16)


def dot(a, b, over):
    return lax.dot_general(a, b, (((over[0],), (over[1],)), ((), ())), preferred_element_type=F32)


def columns(row):
    return jnp.transpose(jnp.broadcast_to(row, (LANES, VARS)))


def decode_kernel(me_ref, held_ref, core_ref, x_hbm, w_hbm, b_hbm, out_ref, keep_ref, send_ref, w_ref, b_ref, sems, more):
    first = [
        pltpu.make_async_copy(w_hbm, w_ref, more.at[0]),
        pltpu.make_async_copy(b_hbm, b_ref, more.at[1]),
    ]
    for copy in first:
        copy.start()
    core = core_ref[0]
    half = keep_ref.shape[0]
    jobs = []
    for part, (to_ref, side) in enumerate(((send_ref, 1 - core), (keep_ref, core))):
        source = pl.ds(pl.multiple_of(side * half, BLOCK), half)
        copy = pltpu.make_async_copy(x_hbm.at[source], to_ref, sems.at[part])
        copy.start()
        jobs.append((copy, to_ref, side))
    for copy in first:
        copy.wait()
    wh, wl = split(w_ref[...])
    both = jnp.concatenate([wh, wl], 0)
    bias = columns(b_ref[...])
    for copy, to_ref, side in jobs:
        copy.wait()
        xh, xl = split(to_ref[...])
        f = dot(both, xh, (1, 1))
        f = f[:VARS] + f[VARS:] + dot(wh, xl, (1, 1))
        for j in range(half // LANES):
            out_ref[2 * j + side] = f[:, j * LANES : (j + 1) * LANES] + bias


def crps_kernel(at_ref, f_ref, t_ref, a_ref, v_ref, grad_ref, extra_ref):
    area = a_ref[pl.ds(at_ref[0], 1), :]
    scale = columns(v_ref[...]) * area
    sums = []
    loss = jnp.zeros((8, LANES), F32)
    for r in range(0, VARS, 8):
        rows = slice(r, r + 8)
        t = t_ref[rows, :]
        f = [f_ref[m, rows, :] for m in range(MEMBERS)]
        slope = [None] * MEMBERS
        near = jnp.zeros((8, LANES), F32)
        pairs = jnp.zeros((8, LANES), F32)
        total = [jnp.zeros((8, LANES), F32) for _ in range(MEMBERS)]
        for i in range(MEMBERS):
            d = f[i] - t
            q = d * d + SMOOTHING * SMOOTHING
            inv = lax.rsqrt(q)
            near = near + q * inv
            slope[i] = d * inv
            for j in range(i + 1, MEMBERS):
                d = f[i] - f[j]
                q = d * d + SMOOTHING * SMOOTHING
                inv = lax.rsqrt(q)
                pairs = pairs + q * inv
                s = d * inv
                total[i] = total[i] + s
                total[j] = total[j] - s
        norm = 1.0 / (MEMBERS * (MEMBERS - 1))
        here = scale[rows]
        loss = loss + here * (near * (1.0 / MEMBERS) - pairs * norm)
        fsum = jnp.zeros((8, LANES), F32)
        for m in range(MEMBERS):
            g = here * (slope[m] * (1.0 / MEMBERS) - total[m] * norm)
            grad_ref[m, rows, :] = g
            fsum = fsum + g
        sums.append(fsum)
    extra_ref[...] = jnp.zeros((EXTRA, LANES), F32)
    bias = jnp.sum(jnp.transpose(jnp.concatenate(sums, 0)), 0, keepdims=True)
    extra_ref[0:1, 0:VARS] = bias
    extra_ref[1:2, :] = jnp.sum(loss, 0, keepdims=True)
    extra_ref[2:3, :] = jnp.sum(a_ref[...], 0, keepdims=True)


def weight_columns(core, side, g_ref, keep_ref, got_ref, e_ref, out_ref):
    columns = pl.ds(pl.multiple_of(side * HALF, HALF), HALF)
    acc = jnp.zeros((VARS, HALF), F32)
    for x_ref, whose in ((keep_ref, core), (got_ref, 1 - core)):
        for i in range(x_ref.shape[0] // BLOCK):
            g = jnp.concatenate([g_ref[i * CHUNKS + j, whose] for j in range(CHUNKS)], 1)
            gh, gl = split(g)
            xh, xl = split(x_ref[i * BLOCK : (i + 1) * BLOCK, columns])
            both = dot(jnp.concatenate([gh, gl], 0), xh, (1, 0))
            acc = acc + (both[:VARS] + both[VARS:] + dot(gh, xl, (1, 0)))
    for i in range(HALF // LANES):
        out_ref[i * VARS : (i + 1) * VARS, :] = acc[:, i * LANES : (i + 1) * LANES]
    out_ref[ROWS:SUMS, :] = e_ref[...]


def weight_other_kernel(c_ref, h_ref, g_ref, keep_ref, got_ref, e_ref, out_ref):
    weight_columns(c_ref[0], 1 - h_ref[0], g_ref, keep_ref, got_ref, e_ref, out_ref)


def weight_own_kernel(c_ref, h_ref, g_ref, keep_ref, got_ref, e_ref, out_ref, send_ref):
    core = c_ref[0]
    weight_columns(core, h_ref[0], g_ref, keep_ref, got_ref, e_ref, out_ref)
    for i in range(g_ref.shape[0]):
        send_ref[i] = g_ref[i, 1 - core]


def pair_kernel(a_ref, b_ref, *refs):
    out_ref = refs[-1]
    out_ref[...] = a_ref[...] + b_ref[...]


def quad_kernel(a_ref, b_ref, c_ref, d_ref, out_ref):
    out_ref[...] = (a_ref[...] + b_ref[...]) + (c_ref[...] + d_ref[...])


def latent_kernel(nodes, c_ref, g_ref, got_ref, w_ref, e_ref, out_hbm, out_ref, sems):
    core = c_ref[0]
    inv = float(nodes * MEMBERS) / jnp.sum(e_ref[ROWS + 2 : ROWS + 3, :], 1, keepdims=True)
    wh, wl = split(w_ref[...])
    w = jnp.concatenate([wh, wh, wl], 0)
    half = out_ref.shape[0] // 2
    copies = []
    for part, side in enumerate((core, 1 - core)):
        for start, size in ((0, LANES), (LANES, half // 2 - LANES), (half // 2, half // 2)) if part == 0 else ((0, half // 2), (half // 2, half // 2)):
            chips = range(start // LANES, (start + size) // LANES)
            g = [g_ref[k, core] if part == 0 else got_ref[k] for k in chips]
            gh, gl = split(jnp.concatenate([a * inv for a in g], 1))
            rows = pl.ds(part * half + start, size)
            out_ref[rows, :] = dot(jnp.concatenate([gh, gl, gh], 0), w, (0, 0))
            to = pl.ds(pl.multiple_of(side * half, BLOCK) + start, size)
            copies.append(pltpu.make_async_copy(out_ref.at[rows], out_hbm.at[to], sems.at[len(copies)]))
            copies[-1].start()
    for copy in copies:
        copy.wait()


def join_kernel(c_ref, mine_ref, theirs_ref, out_ref, loss_ref, bias_ref):
    first = c_ref[0] == 0
    extra = mine_ref[ROWS:, :]
    inv = float(MEMBERS) / jnp.sum(extra[2:3], 1, keepdims=True)
    for i in range(HALF // LANES):
        rows = slice(i * VARS, (i + 1) * VARS)
        mine, theirs = mine_ref[rows, :] * inv, theirs_ref[rows, :] * inv
        out_ref[:, i * LANES : (i + 1) * LANES] = jnp.where(first, mine, theirs)
        out_ref[:, HALF + i * LANES : HALF + (i + 1) * LANES] = jnp.where(first, theirs, mine)
    bias_ref[...] = extra[0:1, :VARS] * inv
    loss_ref[...] = jnp.sum(extra[1:2], 1, keepdims=True) * inv


NEAR = {0: 1, 1: 0, 2: 3, 3: 2}
FAR = {0: 3, 3: 0, 1: 2, 2: 1}
PAIRINGS = {"x1": (1, NEAR), "x2": (1, FAR), "y1": (3, NEAR), "y2": (3, FAR), "z1": (4, NEAR), "z2": (4, FAR), "zl": (0, {0: 1, 1: 0})}


def trade(a, names):
    sizes = [lax.axis_size(axis) for axis in MEMBER + GRID]
    places = list(itertools.product(*[range(n) for n in sizes]))
    number = {place: i for i, place in enumerate(places)}
    pairs = []
    for place in places:
        to = list(place)
        for name in names:
            axis, pairing = PAIRINGS[name]
            to[axis] = pairing[to[axis]]
            to[2] = 1 - to[2]
        pairs.append((number[place], number[tuple(to)]))
    return lax.ppermute(a, MEMBER + GRID, pairs)


def add_round(a, names, *after):
    if len(names) == 1:
        others = [trade(a, names)]
        kernel = pair_kernel
    else:
        others = [trade(a, names[:1]), trade(a, names[1:]), trade(a, names)]
        kernel = quad_kernel
    return pl.pallas_call(kernel, out_shape=shape(SUMS, LANES), compiler_params=params(16))(a, *others, *after)


def whole(shape):
    return pl.BlockSpec(shape, lambda *_: (0,) * len(shape))


def shape(*s):
    return jax.ShapeDtypeStruct(s, F32)


def body(latent, dec_weight, dec_bias, target, area, var_weight):
    slab = area.shape[0]
    nodes = slab * lax.axis_size("y") * lax.axis_size("zh")
    steps = slab // BLOCK
    half = slab // 2
    chips = MEMBERS // 2
    x = latent.reshape(slab, LATENT)
    wt = dec_weight.T
    core = lax.axis_index("c").astype(jnp.int32).reshape(1)
    at = core * chips + lax.axis_index(("zl", "x")).astype(jnp.int32).reshape(1)
    held = (core + sum(lax.axis_index(axis) for axis in ("zl", "x", "y", "zh"))).astype(jnp.int32) & 1
    swap = [(0, 1), (1, 0)]

    fields, keep, send = pl.pallas_call(
        decode_kernel,
        out_shape=(shape(MEMBERS, VARS, LANES), shape(half, LATENT), shape(half, LATENT)),
        in_specs=[SMEM, SMEM, SMEM, HBM, HBM, HBM],
        out_specs=(VMEM, VMEM, VMEM),
        scratch_shapes=[
            pltpu.VMEM((VARS, LATENT), F32),
            pltpu.VMEM((1, VARS), F32),
            pltpu.SemaphoreType.DMA((2,)),
            pltpu.SemaphoreType.DMA((2,)),
        ],
        compiler_params=params(24),
    )(at, held, core, in_hbm(x), in_hbm(wt), in_hbm(dec_bias.reshape(1, VARS)))

    got = lax.ppermute(send, "c", swap)
    fields = lax.all_to_all(fields, MEMBER, 0, 0)

    grads, extra = pl.pallas_call(
        crps_kernel,
        out_shape=(shape(MEMBERS, VARS, LANES), shape(EXTRA, LANES)),
        grid_spec=pltpu.PrefetchScalarGridSpec(
            num_scalar_prefetch=1,
            grid=(1,),
            in_specs=[
                whole((MEMBERS, VARS, LANES)),
                pl.BlockSpec((VARS, LANES), lambda i, at: (0, at[0])),
                whole((slab // LANES, LANES)),
                whole((1, VARS)),
            ],
            out_specs=(whole((MEMBERS, VARS, LANES)), whole((EXTRA, LANES))),
        ),
        compiler_params=params(16),
    )(at, fields, target, area.reshape(slab // LANES, LANES), var_weight.reshape(1, VARS))

    grads = lax.all_to_all(grads.reshape(chips, 2, VARS, LANES), ("zl", "x"), 0, 0)

    def weight(kernel, *outs):
        return pl.pallas_call(
            kernel,
            out_shape=outs,
            in_specs=[SMEM, SMEM, VMEM, VMEM, VMEM, VMEM],
            out_specs=(VMEM,) * len(outs),
            compiler_params=params(24),
            cost_estimate=pl.CostEstimate(flops=6 * slab * VARS * HALF, bytes_accessed=4 * slab * HALF, transcendentals=0),
        )(core, held, grads, keep, got, extra)

    (other,) = weight(weight_other_kernel, shape(SUMS, LANES))
    came = lax.ppermute(other, "c", swap)
    own, send = weight(weight_own_kernel, shape(SUMS, LANES), shape(chips, VARS, LANES))
    rest = lax.ppermute(send, "c", swap)
    sums = pl.pallas_call(pair_kernel, out_shape=shape(SUMS, LANES), compiler_params=params(16))(own, came)
    sums = add_round(sums, ("x1", "zl"))
    sums = add_round(sums, ("x2", "y2"))
    sums = add_round(sums, ("y1", "z1"))
    sums = add_round(sums, ("z2",))
    theirs = lax.ppermute(sums, "c", swap)

    grad_latent = pl.pallas_call(
        lambda *refs: latent_kernel(nodes, *refs),
        out_shape=shape(slab, LATENT),
        in_specs=[SMEM, VMEM, VMEM, VMEM, VMEM],
        out_specs=HBM,
        scratch_shapes=[pltpu.VMEM((slab, LATENT), F32), pltpu.SemaphoreType.DMA((steps + 1,))],
        compiler_params=params(24),
        cost_estimate=pl.CostEstimate(flops=6 * slab * VARS * LATENT, bytes_accessed=4 * slab * LATENT, transcendentals=0),
    )(core, grads, rest, wt, sums)

    grad_weight, loss, bias = pl.pallas_call(
        join_kernel,
        out_shape=(shape(VARS, LATENT), shape(1, 1), shape(1, VARS)),
        in_specs=[SMEM, VMEM, VMEM],
        out_specs=(VMEM, VMEM, VMEM),
        compiler_params=params(16),
    )(held, sums, theirs)
    return loss.reshape(()), grad_latent[None], grad_weight.T, bias.reshape(VARS)


def solution(mesh):
    shaped = Mesh(mesh.devices.reshape(2, 4, 2, 4, 4), MEMBER + GRID)
    return jax.shard_map(
        body,
        mesh=shaped,
        in_specs=(P(MEMBER, GRID, None), P(), P(), P(None, GRID), P(GRID), P()),
        out_specs=(P(), P(MEMBER, GRID, None), P(), P()),
        check_vma=False,
    )
```

```python
import functools
import itertools

import jax
import jax.numpy as jnp
from jax import lax
from jax.experimental import pallas as pl
from jax.experimental.pallas import tpu as pltpu
from jax.sharding import Mesh, PartitionSpec as P

MEMBERS = 16
LATENT = 512
VARS = 32
SMOOTHING = 0.1
LANES = 128
BLOCK = 512
CHUNKS = BLOCK // LANES
HALF = LATENT // 2
ROWS = VARS * HALF // LANES
EXTRA = 8
SUMS = ROWS + EXTRA
MEMBER = ("zl", "x", "c")
GRID = ("y", "zh")
F32 = jnp.float32
BF16 = jnp.bfloat16
VMEM = pl.BlockSpec(memory_space=pltpu.VMEM)
SMEM = pl.BlockSpec(memory_space=pltpu.SMEM)
HBM = pl.BlockSpec(memory_space=pltpu.HBM)


def in_hbm(a):
    return pltpu.with_memory_space_constraint(a, pltpu.HBM)


def params(mib):
    return pltpu.CompilerParams(vmem_limit_bytes=mib * 1024 * 1024)


def split(a):
    hi = a.astype(BF16)
    return hi, (a - hi.astype(F32)).astype(BF16)


def dot(a, b, over):
    return lax.dot_general(a, b, (((over[0],), (over[1],)), ((), ())), preferred_element_type=F32)


def columns(row):
    return jnp.transpose(jnp.broadcast_to(row, (LANES, VARS)))


def decode_kernel(me_ref, held_ref, core_ref, x_hbm, w_hbm, b_hbm, out_ref, keep_ref, send_ref, w_ref, b_ref, sems, more):
    first = [
        pltpu.make_async_copy(w_hbm, w_ref, more.at[0]),
        pltpu.make_async_copy(b_hbm, b_ref, more.at[1]),
    ]
    for copy in first:
        copy.start()
    core = core_ref[0]
    half = keep_ref.shape[0]
    jobs = []
    for part, (to_ref, side) in enumerate(((send_ref, 1 - core), (keep_ref, core))):
        source = pl.ds(pl.multiple_of(side * half, BLOCK), half)
        copy = pltpu.make_async_copy(x_hbm.at[source], to_ref, sems.at[part])
        copy.start()
        jobs.append((copy, to_ref, side))
    for copy in first:
        copy.wait()
    wh, wl = split(w_ref[...])
    both = jnp.concatenate([wh, wl], 0)
    bias = columns(b_ref[...])
    for copy, to_ref, side in jobs:
        copy.wait()
        xh, xl = split(to_ref[...])
        f = dot(both, xh, (1, 1))
        f = f[:VARS] + f[VARS:] + dot(wh, xl, (1, 1))
        for j in range(half // LANES):
            out_ref[2 * j + side] = f[:, j * LANES : (j + 1) * LANES] + bias


def crps_kernel(at_ref, f_ref, t_ref, a_ref, v_ref, grad_ref, extra_ref):
    area = a_ref[pl.ds(at_ref[0], 1), :]
    scale = columns(v_ref[...]) * area
    sums = []
    loss = jnp.zeros((8, LANES), F32)
    for r in range(0, VARS, 8):
        rows = slice(r, r + 8)
        t = t_ref[rows, :]
        f = [f_ref[m, rows, :] for m in range(MEMBERS)]
        slope = [None] * MEMBERS
        near = jnp.zeros((8, LANES), F32)
        pairs = jnp.zeros((8, LANES), F32)
        total = [jnp.zeros((8, LANES), F32) for _ in range(MEMBERS)]
        for i in range(MEMBERS):
            d = f[i] - t
            q = d * d + SMOOTHING * SMOOTHING
            inv = lax.rsqrt(q)
            near = near + q * inv
            slope[i] = d * inv
            for j in range(i + 1, MEMBERS):
                d = f[i] - f[j]
                q = d * d + SMOOTHING * SMOOTHING
                inv = lax.rsqrt(q)
                pairs = pairs + q * inv
                s = d * inv
                total[i] = total[i] + s
                total[j] = total[j] - s
        norm = 1.0 / (MEMBERS * (MEMBERS - 1))
        here = scale[rows]
        loss = loss + here * (near * (1.0 / MEMBERS) - pairs * norm)
        fsum = jnp.zeros((8, LANES), F32)
        for m in range(MEMBERS):
            g = here * (slope[m] * (1.0 / MEMBERS) - total[m] * norm)
            grad_ref[m, rows, :] = g
            fsum = fsum + g
        sums.append(fsum)
    extra_ref[...] = jnp.zeros((EXTRA, LANES), F32)
    bias = jnp.sum(jnp.transpose(jnp.concatenate(sums, 0)), 0, keepdims=True)
    extra_ref[0:1, 0:VARS] = bias
    extra_ref[1:2, :] = jnp.sum(loss, 0, keepdims=True)
    extra_ref[2:3, :] = jnp.sum(a_ref[...], 0, keepdims=True)


def weight_columns(core, side, g_ref, keep_ref, got_ref, e_ref, out_ref):
    columns = pl.ds(pl.multiple_of(side * HALF, HALF), HALF)
    acc = jnp.zeros((VARS, HALF), F32)
    for x_ref, whose in ((keep_ref, core), (got_ref, 1 - core)):
        gh, gl = split(jnp.concatenate([g_ref[i, whose] for i in range(g_ref.shape[0])], 1))
        xh, xl = split(x_ref[:, columns])
        both = dot(jnp.concatenate([gh, gl], 0), xh, (1, 0))
        acc = acc + (both[:VARS] + both[VARS:] + dot(gh, xl, (1, 0)))
    for i in range(HALF // LANES):
        out_ref[i * VARS : (i + 1) * VARS, :] = acc[:, i * LANES : (i + 1) * LANES]
    out_ref[ROWS:SUMS, :] = e_ref[...]


def weight_other_kernel(c_ref, h_ref, g_ref, keep_ref, got_ref, e_ref, out_ref):
    weight_columns(c_ref[0], 1 - h_ref[0], g_ref, keep_ref, got_ref, e_ref, out_ref)


def weight_own_kernel(c_ref, h_ref, g_ref, keep_ref, got_ref, e_ref, out_ref, send_ref):
    core = c_ref[0]
    weight_columns(core, h_ref[0], g_ref, keep_ref, got_ref, e_ref, out_ref)
    for i in range(g_ref.shape[0]):
        send_ref[i] = g_ref[i, 1 - core]


def pair_kernel(a_ref, b_ref, *refs):
    out_ref = refs[-1]
    out_ref[...] = a_ref[...] + b_ref[...]


def quad_kernel(a_ref, b_ref, c_ref, d_ref, out_ref):
    out_ref[...] = (a_ref[...] + b_ref[...]) + (c_ref[...] + d_ref[...])


def latent_kernel(nodes, c_ref, g_ref, got_ref, w_ref, e_ref, out_hbm, out_ref, sems):
    core = c_ref[0]
    inv = float(nodes * MEMBERS) / jnp.sum(e_ref[ROWS + 2 : ROWS + 3, :], 1, keepdims=True)
    wh, wl = split(w_ref[...])
    w = jnp.concatenate([wh, wh, wl], 0)
    half = out_ref.shape[0] // 2
    copies = []
    for part, side in enumerate((core, 1 - core)):
        for start, size in ((0, LANES), (LANES, half // 2 - LANES), (half // 2, half // 2)) if part == 0 else ((0, half // 2), (half // 2, half // 2)):
            chips = range(start // LANES, (start + size) // LANES)
            g = [g_ref[k, core] if part == 0 else got_ref[k] for k in chips]
            gh, gl = split(jnp.concatenate([a * inv for a in g], 1))
            rows = pl.ds(part * half + start, size)
            out_ref[rows, :] = dot(jnp.concatenate([gh, gl, gh], 0), w, (0, 0))
            to = pl.ds(pl.multiple_of(side * half, BLOCK) + start, size)
            copies.append(pltpu.make_async_copy(out_ref.at[rows], out_hbm.at[to], sems.at[len(copies)]))
            copies[-1].start()
    for copy in copies:
        copy.wait()


def join_kernel(c_ref, mine_ref, theirs_ref, out_ref, loss_ref, bias_ref):
    first = c_ref[0] == 0
    extra = mine_ref[ROWS:, :]
    inv = float(MEMBERS) / jnp.sum(extra[2:3], 1, keepdims=True)
    for i in range(HALF // LANES):
        rows = slice(i * VARS, (i + 1) * VARS)
        mine, theirs = mine_ref[rows, :] * inv, theirs_ref[rows, :] * inv
        out_ref[:, i * LANES : (i + 1) * LANES] = jnp.where(first, mine, theirs)
        out_ref[:, HALF + i * LANES : HALF + (i + 1) * LANES] = jnp.where(first, theirs, mine)
    bias_ref[...] = extra[0:1, :VARS] * inv
    loss_ref[...] = jnp.sum(extra[1:2], 1, keepdims=True) * inv


NEAR = {0: 1, 1: 0, 2: 3, 3: 2}
FAR = {0: 3, 3: 0, 1: 2, 2: 1}
PAIRINGS = {"x1": (1, NEAR), "x2": (1, FAR), "y1": (3, NEAR), "y2": (3, FAR), "z1": (4, NEAR), "z2": (4, FAR), "zl": (0, {0: 1, 1: 0})}


def trade(a, names):
    sizes = [lax.axis_size(axis) for axis in MEMBER + GRID]
    places = list(itertools.product(*[range(n) for n in sizes]))
    number = {place: i for i, place in enumerate(places)}
    pairs = []
    for place in places:
        to = list(place)
        for name in names:
            axis, pairing = PAIRINGS[name]
            to[axis] = pairing[to[axis]]
            to[2] = 1 - to[2]
        pairs.append((number[place], number[tuple(to)]))
    return lax.ppermute(a, MEMBER + GRID, pairs)


def add_round(a, names, *after):
    if len(names) == 1:
        others = [trade(a, names)]
        kernel = pair_kernel
    else:
        others = [trade(a, names[:1]), trade(a, names[1:]), trade(a, names)]
        kernel = quad_kernel
    return pl.pallas_call(kernel, out_shape=shape(SUMS, LANES), compiler_params=params(16))(a, *others, *after)


def whole(shape):
    return pl.BlockSpec(shape, lambda *_: (0,) * len(shape))


def shape(*s):
    return jax.ShapeDtypeStruct(s, F32)


def body(latent, dec_weight, dec_bias, target, area, var_weight):
    slab = area.shape[0]
    nodes = slab * lax.axis_size("y") * lax.axis_size("zh")
    steps = slab // BLOCK
    half = slab // 2
    chips = MEMBERS // 2
    x = latent.reshape(slab, LATENT)
    wt = dec_weight.T
    core = lax.axis_index("c").astype(jnp.int32).reshape(1)
    at = core * chips + lax.axis_index(("zl", "x")).astype(jnp.int32).reshape(1)
    held = (core + sum(lax.axis_index(axis) for axis in ("zl", "x", "y", "zh"))).astype(jnp.int32) & 1
    swap = [(0, 1), (1, 0)]

    fields, keep, send = pl.pallas_call(
        decode_kernel,
        out_shape=(shape(MEMBERS, VARS, LANES), shape(half, LATENT), shape(half, LATENT)),
        in_specs=[SMEM, SMEM, SMEM, HBM, HBM, HBM],
        out_specs=(VMEM, VMEM, VMEM),
        scratch_shapes=[
            pltpu.VMEM((VARS, LATENT), F32),
            pltpu.VMEM((1, VARS), F32),
            pltpu.SemaphoreType.DMA((2,)),
            pltpu.SemaphoreType.DMA((2,)),
        ],
        compiler_params=params(24),
    )(at, held, core, in_hbm(x), in_hbm(wt), in_hbm(dec_bias.reshape(1, VARS)))

    got = lax.ppermute(send, "c", swap)
    fields = lax.all_to_all(fields, MEMBER, 0, 0)

    grads, extra = pl.pallas_call(
        crps_kernel,
        out_shape=(shape(MEMBERS, VARS, LANES), shape(EXTRA, LANES)),
        grid_spec=pltpu.PrefetchScalarGridSpec(
            num_scalar_prefetch=1,
            grid=(1,),
            in_specs=[
                whole((MEMBERS, VARS, LANES)),
                pl.BlockSpec((VARS, LANES), lambda i, at: (0, at[0])),
                whole((slab // LANES, LANES)),
                whole((1, VARS)),
            ],
            out_specs=(whole((MEMBERS, VARS, LANES)), whole((EXTRA, LANES))),
        ),
        compiler_params=params(16),
    )(at, fields, target, area.reshape(slab // LANES, LANES), var_weight.reshape(1, VARS))

    grads = lax.all_to_all(grads.reshape(chips, 2, VARS, LANES), ("zl", "x"), 0, 0)

    def weight(kernel, *outs):
        return pl.pallas_call(
            kernel,
            out_shape=outs,
            in_specs=[SMEM, SMEM, VMEM, VMEM, VMEM, VMEM],
            out_specs=(VMEM,) * len(outs),
            compiler_params=params(24),
            cost_estimate=pl.CostEstimate(flops=6 * slab * VARS * HALF, bytes_accessed=4 * slab * HALF, transcendentals=0),
        )(core, held, grads, keep, got, extra)

    (other,) = weight(weight_other_kernel, shape(SUMS, LANES))
    came = lax.ppermute(other, "c", swap)
    own, send = weight(weight_own_kernel, shape(SUMS, LANES), shape(chips, VARS, LANES))
    rest = lax.ppermute(send, "c", swap)
    sums = pl.pallas_call(pair_kernel, out_shape=shape(SUMS, LANES), compiler_params=params(16))(own, came)
    sums = add_round(sums, ("x1", "zl"))
    sums = add_round(sums, ("x2", "y2"))
    sums = add_round(sums, ("y1", "z1"))
    sums = add_round(sums, ("z2",))
    theirs = lax.ppermute(sums, "c", swap)

    grad_latent = pl.pallas_call(
        lambda *refs: latent_kernel(nodes, *refs),
        out_shape=shape(slab, LATENT),
        in_specs=[SMEM, VMEM, VMEM, VMEM, VMEM],
        out_specs=HBM,
        scratch_shapes=[pltpu.VMEM((slab, LATENT), F32), pltpu.SemaphoreType.DMA((steps + 1,))],
        compiler_params=params(24),
        cost_estimate=pl.CostEstimate(flops=6 * slab * VARS * LATENT, bytes_accessed=4 * slab * LATENT, transcendentals=0),
    )(core, grads, rest, wt, sums)

    grad_weight, loss, bias = pl.pallas_call(
        join_kernel,
        out_shape=(shape(VARS, LATENT), shape(1, 1), shape(1, VARS)),
        in_specs=[SMEM, VMEM, VMEM],
        out_specs=(VMEM, VMEM, VMEM),
        compiler_params=params(16),
    )(held, sums, theirs)
    return loss.reshape(()), grad_latent[None], grad_weight.T, bias.reshape(VARS)


def solution(mesh):
    shaped = Mesh(mesh.devices.reshape(2, 4, 2, 4, 4), MEMBER + GRID)
    return jax.shard_map(
        body,
        mesh=shaped,
        in_specs=(P(MEMBER, GRID, None), P(), P(), P(None, GRID), P(GRID), P()),
        out_specs=(P(), P(MEMBER, GRID, None), P(), P()),
        check_vma=False,
    )
```
